32 devices in a mesh: fsdp: 8 (over z, x), seq: 4 (over y, core).
Axes of the slice: x: 2, y: 2, z: 4, core: 2. Of those that a mesh axis runs over, the one named last changes fastest.
Arguments:
- inputs: bfloat16 [16384, 768], P(('fsdp', 'seq')), may hold values from -6 to 6
- cotangent: bfloat16 [16384, 768], P(('fsdp', 'seq')), may hold values from -6 to 6
- first_gain: bfloat16 [768], P('fsdp'), may hold values from 0.5 to 1.5
- first_bias: bfloat16 [768], P('fsdp'), may hold values from -1.5 to 1.5
- triple_weight: bfloat16 [768, 2304], P(None, 'fsdp'), may hold values from -0.3125 to 0.3125
- query_bias: bfloat16 [768], P('fsdp'), may hold values from -1.5 to 1.5
- value_bias: bfloat16 [768], P('fsdp'), may hold values from -1.5 to 1.5
- out_weight: bfloat16 [768, 768], P(None, 'fsdp'), may hold values from -0.875 to 0.875
- out_bias: bfloat16 [768], P('fsdp'), may hold values from -1.5 to 1.5
- second_gain: bfloat16 [768], P('fsdp'), may hold values from 0.5 to 1.5
- second_bias: bfloat16 [768], P('fsdp'), may hold values from -1.5 to 1.5
- expand_weight: bfloat16 [768, 3072], P(None, 'fsdp'), may hold values from -0.21875 to 0.21875
- expand_bias: bfloat16 [3072], P('fsdp'), may hold values from -1.5 to 1.5
- reduce_weight: bfloat16 [3072, 768], P(None, 'fsdp'), may hold values from -0.109375 to 0.109375
- reduce_bias: bfloat16 [768], P('fsdp'), may hold values from -1.5 to 1.5
Outputs:
- output: bfloat16 [16384, 768], P(('fsdp', 'seq'))
- grad_inputs: bfloat16 [16384, 768], P(('fsdp', 'seq'))
- grad_first_gain: float32 [768], P('fsdp')
- grad_first_bias: float32 [768], P('fsdp')
- grad_triple_weight: float32 [768, 2304], P(None, 'fsdp')
- grad_query_bias: float32 [768], P('fsdp')
- grad_value_bias: float32 [768], P('fsdp')
- grad_out_weight: float32 [768, 768], P(None, 'fsdp')
- grad_out_bias: float32 [768], P('fsdp')
- grad_second_gain: float32 [768], P('fsdp')
- grad_second_bias: float32 [768], P('fsdp')
- grad_expand_weight: float32 [768, 3072], P(None, 'fsdp')
- grad_expand_bias: float32 [3072], P('fsdp')
- grad_reduce_weight: float32 [3072, 768], P(None, 'fsdp')
- grad_reduce_bias: float32 [768], P('fsdp')
The draws below stay inside these ranges and needn't reach their ends.
All inputs are finite; a program needn't handle non-finite values.
Results may differ from the reference program's by a relative error of at most 0.017.
Values may be sent and summed in bfloat16 or wider, within the bound.
No kernel may reach another device: no remote copies, remote signals or barrier semaphores. Data moves between devices by JAX's collectives and lax.ppermute only.
A program may use at most 192 MiB of HBM per device.

```python
import jax
import jax.numpy as jnp
from jax import lax

MODEL = 768
HEADS = 12
HEAD_DIM = 64
HIDDEN_SIZE = 3072
LENGTH = 16384
SEQS = 1
TOKENS = 16384


def raised(array, rng, source, target, shards_of, factor):
    owner, partner = [(jnp.arange(array.shape[axis_at]) // (array.shape[axis_at] // shards_of)).reshape([-1 if axis == axis_at else 1 for axis in range(array.ndim)]) for axis_at in (source, target)]
    chosen = jax.random.permutation(rng, shards_of)[partner]
    strong = (owner == chosen) | (owner == (partner + shards_of // 2) % shards_of)
    return jnp.where(strong, factor * array, array)


def shard_levels(key, shape, split, least, largest):
    loudness = 1.0
    for dim, shards_of in split:
        steps = jax.random.uniform(jax.random.fold_in(jax.random.fold_in(key, 6), dim), (shards_of,), jnp.float32, least / len(split), largest / len(split))
        loudness = loudness * jnp.repeat(jnp.exp(steps), shape[dim] // shards_of).reshape((-1,) + (1,) * (len(shape) - 1 - dim))
    return loudness


def centred(stream_key, shape, scale, reach, cuts=(), kind=jnp.bfloat16):
    values = scale * jax.random.normal(stream_key, shape, jnp.float32)
    if cuts:
        values = values * shard_levels(stream_key, shape, cuts, -0.22, 0.18)
    return jnp.clip(values, -reach, reach).astype(kind)


def bell_draw_with(own_key, shape, scale, most, cuts, heavy, held_as=jnp.bfloat16):
    drawn = scale * jax.random.normal(own_key, shape, jnp.float32)
    if cuts:
        drawn = drawn * shard_levels(own_key, shape, cuts, -0.22, 0.18)
    return jnp.clip(raised(drawn, jax.random.fold_in(own_key, 3), *heavy), -most, most).astype(held_as)


def setup_inputs(seed: int = 0) -> dict:
    seeds = jax.random.split(jax.random.key(seed), 16)
    return {
        "inputs": centred(seeds[0], (TOKENS, MODEL), 1.0, 6.0, ((0, 32),)),
        "cotangent": bell_draw_with(seeds[1], (TOKENS, MODEL), 1.0, 6.0, ((0, 32),), (0, 1, 32, 2.75)),
        "first_gain": jnp.clip(0.5 + 1.0 * jax.random.uniform(seeds[2], (MODEL,), jnp.float32) ** shard_levels(seeds[2], (MODEL,), ((0, 8),), -0.2, 0.2), 0.5, 1.5).astype(jnp.bfloat16),
        "first_bias": centred(seeds[3], (MODEL,), 0.3, 1.5, ((0, 8),)),
        "triple_weight": centred(seeds[4], (MODEL, 3 * MODEL), (MODEL // 2) ** -0.5, 0.3125, ((1, 8),)),
        "query_bias": centred(seeds[5], (MODEL,), 0.3, 1.5, ((0, 8),)),
        "value_bias": centred(seeds[6], (MODEL,), 0.3, 1.5, ((0, 8),)),
        "out_weight": centred(seeds[7], (MODEL, MODEL), (MODEL // 16) ** -0.5, 0.875, ((1, 8),)),
        "out_bias": centred(seeds[8], (MODEL,), 0.3, 1.5, ((0, 8),)),
        "second_gain": jnp.clip(0.5 + 1.0 * jax.random.uniform(seeds[9], (MODEL,), jnp.float32) ** shard_levels(seeds[9], (MODEL,), ((0, 8),), -0.2, 0.2), 0.5, 1.5).astype(jnp.bfloat16),
        "second_bias": centred(seeds[10], (MODEL,), 0.3, 1.5, ((0, 8),)),
        "expand_weight": centred(seeds[11], (MODEL, HIDDEN_SIZE), MODEL ** -0.5, 0.21875, ((1, 8),)),
        "expand_bias": centred(seeds[12], (HIDDEN_SIZE,), 0.3, 1.5, ((0, 8),)),
        "reduce_weight": centred(seeds[13], (HIDDEN_SIZE, MODEL), HIDDEN_SIZE ** -0.5, 0.109375, ((1, 8),)),
        "reduce_bias": centred(seeds[14], (MODEL,), 0.3, 1.5, ((0, 8),)),
    }


EPSILON = 1e-05
NEGATIVE = -1e+30
HIGH = lax.Precision.HIGHEST

@jax.custom_vjp
def low(v):
    return lax.optimization_barrier(v.astype(jnp.bfloat16)).astype(jnp.float32)

@jax.custom_vjp
def low_back(v):
    return v

def low_keep(v):
    return (low(v), None)

def low_pass(kept, grad):
    return (grad,)

def back_keep(v):
    return (v, None)

def back_low(kept, grad):
    return (low(grad),)
low.defvjp(low_keep, low_pass)
low_back.defvjp(back_keep, back_low)

def layer_norm(value, gain, bias):
    centre = value - lax.optimization_barrier(jnp.mean(value, axis=-1, keepdims=True))
    spread = lax.optimization_barrier(jnp.mean(centre * centre, axis=-1, keepdims=True))
    return centre * lax.rsqrt(spread + EPSILON) * gain + bias

def smooth_gelu(value):
    return 0.5 * value * (1.0 + jnp.tanh(0.7978845608028654 * (value + 0.044715 * value * value * value)))

def matmul(left, right):
    return jnp.dot(left, right, precision=HIGH, preferred_element_type=jnp.float32)

def sequence_attention(queries, keys, values):
    block = min(512, LENGTH)
    scale = HEAD_DIM ** (-0.5)
    positions = jnp.arange(LENGTH, dtype=jnp.int32)

    def one_block(first):
        rows = lax.dynamic_slice_in_dim(queries, first, block, 0)
        scores = jnp.einsum('qhd,khd->hqk', rows, keys, precision=HIGH) * scale
        scores = low_back(scores)
        here = first + jnp.arange(block, dtype=jnp.int32)
        scores = jnp.where(positions[None, None, :] <= here[None, :, None], scores, NEGATIVE)
        top = lax.optimization_barrier(jnp.max(scores, axis=-1, keepdims=True))
        weights = jnp.exp(scores - top)
        probs = weights / lax.optimization_barrier(jnp.sum(weights, axis=-1, keepdims=True))
        return jnp.einsum('hqk,khd->qhd', low(probs), values, precision=HIGH)
    firsts = jnp.arange(LENGTH // block, dtype=jnp.int32) * block
    outputs = lax.map(jax.checkpoint(one_block), firsts)
    return outputs.reshape(LENGTH, HEADS, HEAD_DIM)

def one_sequence(parts):
    return sequence_attention(parts[:, 0], parts[:, 1], parts[:, 2])

def layer(params, inputs):
    first_gain, first_bias, triple_weight, query_bias, value_bias, out_weight, out_bias, second_gain, second_bias, expand_weight, expand_bias, reduce_weight, reduce_bias = params
    normed1 = low(layer_norm(inputs, first_gain, first_bias))
    blank = jnp.zeros_like(query_bias)
    mixed = matmul(normed1, triple_weight) + jnp.concatenate([query_bias, blank, value_bias])
    mixed = low_back(low(mixed))
    parts = mixed.reshape(SEQS, LENGTH, 3, HEADS, HEAD_DIM)
    attended = lax.map(one_sequence, parts)
    attended = low_back(low(attended.reshape(TOKENS, MODEL)))
    middle = inputs + low_back(matmul(attended, out_weight) + out_bias)
    normed2 = low(layer_norm(middle, second_gain, second_bias))
    pre = low_back(matmul(normed2, expand_weight) + expand_bias)
    act = low(smooth_gelu(pre))
    return middle + matmul(act, reduce_weight) + reduce_bias

def reference(inputs, cotangent, first_gain, first_bias, triple_weight, query_bias, value_bias, out_weight, out_bias, second_gain, second_bias, expand_weight, expand_bias, reduce_weight, reduce_bias):
    params = (first_gain.astype(jnp.float32), first_bias.astype(jnp.float32), triple_weight.astype(jnp.float32), query_bias.astype(jnp.float32), value_bias.astype(jnp.float32), out_weight.astype(jnp.float32), out_bias.astype(jnp.float32), second_gain.astype(jnp.float32), second_bias.astype(jnp.float32), expand_weight.astype(jnp.float32), expand_bias.astype(jnp.float32), reduce_weight.astype(jnp.float32), reduce_bias.astype(jnp.float32))
    result, pullback = jax.vjp(layer, params, inputs.astype(jnp.float32))
    grads, grad_in = pullback(cotangent.astype(jnp.float32))
    return (result.astype(jnp.bfloat16), grad_in.astype(jnp.bfloat16), grads[0], grads[1], grads[2], grads[3], grads[4], grads[5], grads[6], grads[7], grads[8], grads[9], grads[10], grads[11], grads[12])
```

```python
import functools

import jax
import jax.numpy as jnp
from jax import lax
from jax.experimental import pallas as pl
from jax.experimental.pallas import tpu as pltpu
from jax.sharding import Mesh
from jax.sharding import PartitionSpec as P

HEADS = 12
HEAD_DIM = 64
GROUP = 8
EPSILON = 1e-05
NEG = -1e30
LOG2E = 1.4426950408889634
CH = 512
BF = jnp.bfloat16
F32 = jnp.float32
WEIGHT_AXES = ("g", "z", "x")
RING = ("x", "y", "c")
ALL = ("g", "z", "x", "y", "c")
def dotf(a,b): return lax.dot_general(a,b,(((1,),(0,)),((),())),preferred_element_type=jnp.float32)

def fill(kv_ref, kva, vt):
    n=kv_ref.shape[0]
    def body(i,_):
        rows=pl.ds(pl.multiple_of(i*CH,CH),CH)
        blk=kv_ref[rows,:]
        lane=lax.broadcasted_iota(jnp.int32,(CH,128),1)
        one=jnp.where((lane>=64)&(lane<67),1.0,0.0).astype(jnp.bfloat16)
        kva[rows,0:128]=blk
        kva[rows,128:256]=jnp.where(lane<64,blk,one)
        t=blk.T
        cols=pl.ds(pl.multiple_of(i*CH,CH),CH)
        if vt.shape[0]==80:
            vt[0:64,cols]=t[64:128]
            vt[64:80,cols]=jnp.ones((16,CH),jnp.bfloat16)
        else:
            vt[:,cols]=t[0:64]
        return 0
    lax.fori_loop(0,n//CH,body,0)

def pos(j,strips):
    return pl.multiple_of((lax.rem(j,8)*strips+lax.div(j,8))*CH,CH)

def fwd_kernel(strips, unroll, r_ref, qt_ref, kv_ref, ot_ref, lse_ref, kva, vt, m_s, acc):
    r=r_ref[0]; i=pl.program_id(0)
    @pl.when(i==0)
    def _(): fill(kv_ref,kva,vt)
    qt=qt_ref[...]
    m_s[...]=jnp.full(m_s.shape,NEG,jnp.float32)
    acc[...]=jnp.zeros(acc.shape,jnp.float32)
    def step(js,diag):
        ss=[]
        for j in js:
            p0=pos(j,strips)
            s=dotf(kva[pl.ds(p0,CH),:],qt)
            ss.append(s)
        if diag:
            ki=lax.broadcasted_iota(jnp.int32,(CH,CH),0); qi=lax.broadcasted_iota(jnp.int32,(CH,CH),1)
            ss[-1]=jnp.where(ki<=qi,ss[-1],NEG)
        m0=m_s[...]
        m1=m0
        for s in ss: m1=jnp.maximum(m1,jnp.max(s,axis=0,keepdims=True))
        al=jnp.exp2(m0-m1)
        o=acc[...]*al
        for j,s in zip(js,ss):
            p=jnp.exp2(s-m1).astype(jnp.bfloat16)
            o=o+dotf(vt[:,pl.ds(pos(j,strips),CH)],p)
        acc[...]=o
        m_s[...]=m1
    n=i*8+r
    def body(t,_):
        step([t*unroll+u for u in range(unroll)],False); return 0
    nt=lax.div(n,unroll)
    lax.fori_loop(0,nt,body,0)
    def tail(j,_):
        step([j],False); return 0
    lax.fori_loop(nt*unroll,n,tail,0)
    step([n],True)
    o=acc[...]
    l=o[64:65]
    ot_ref[...]=o[0:64]/l
    lse_ref[...]=jnp.broadcast_to(m_s[...]+jnp.log2(l),lse_ref.shape)

def attend(r,qt,kv,unroll=2):
    n=kv.shape[0]; rows=qt.shape[1]; strips=rows//CH
    return pl.pallas_call(functools.partial(fwd_kernel,strips,unroll),
      grid=(strips,),
      in_specs=[pl.BlockSpec(memory_space=pltpu.SMEM),pl.BlockSpec((256,CH),lambda i:(0,i)),pl.BlockSpec((n,128),lambda i:(0,0))],
      out_specs=[pl.BlockSpec((64,CH),lambda i:(0,i)),pl.BlockSpec((8,CH),lambda i:(0,i))],
      out_shape=[jax.ShapeDtypeStruct((64,rows),jnp.float32),jax.ShapeDtypeStruct((8,rows),jnp.float32)],
      scratch_shapes=[pltpu.VMEM((n,256),jnp.bfloat16),pltpu.VMEM((80,n),jnp.bfloat16),pltpu.VMEM((1,CH),jnp.float32),pltpu.VMEM((80,CH),jnp.float32)],
      compiler_params=pltpu.CompilerParams(vmem_limit_bytes=56*2**20),
      cost_estimate=pl.CostEstimate(flops=20_000_000_000,bytes_accessed=8*2**20,transcendentals=n*rows//2),
    )(r,qt,kv)

def bwd_kernel(strips, r_ref, qt_ref, dot_ref, qn_ref, don_ref, kv_ref, dqt_ref, dkv_ref, kva, kt, dkv, dq):
    r=r_ref[0]; i=pl.program_id(0)
    @pl.when(i==0)
    def _():
        fill(kv_ref,kva,kt)
        def z(t,_):
            dkv[pl.ds(pl.multiple_of(t*CH,CH),CH),:]=jnp.zeros((CH,128),jnp.float32); return 0
        lax.fori_loop(0,dkv.shape[0]//CH,z,0)
    dq[...]=jnp.zeros(dq.shape,jnp.float32)
    def step(j,diag):
        p0=pos(j,strips)
        ks=kva[pl.ds(p0,CH),:]
        s=dotf(ks,qt_ref[...])
        if diag:
            ki=lax.broadcasted_iota(jnp.int32,(CH,CH),0); qi=lax.broadcasted_iota(jnp.int32,(CH,CH),1)
            s=jnp.where(ki<=qi,s,NEG)
        p=jnp.exp2(s)
        dp=dotf(ks,dot_ref[...])
        ds=(p*dp).astype(jnp.bfloat16)
        p=p.astype(jnp.bfloat16)
        dkv[pl.ds(p0,CH),:]+=dotf(p,don_ref[...])+dotf(ds,qn_ref[...])
        dq[...]+=dotf(kt[:,pl.ds(p0,CH)],ds)
    n=i*8+r
    def body(j,_):
        step(j,False); return 0
    lax.fori_loop(0,n,body,0)
    step(n,True)
    dqt_ref[...]=(dq[...]*0.125).astype(dqt_ref.dtype)
    @pl.when(i==strips-1)
    def _():
        def w(t,_):
            rows=pl.ds(pl.multiple_of(t*CH,CH),CH)
            dkv_ref[rows,:]=dkv[rows,:].astype(jnp.bfloat16); return 0
        lax.fori_loop(0,dkv.shape[0]//CH,w,0)

def attend_back(r,qt,dot_,qn,don,kv):
    n=kv.shape[0]; rows=qt.shape[1]; strips=rows//CH
    return pl.pallas_call(functools.partial(bwd_kernel,strips),
      grid=(strips,),
      in_specs=[pl.BlockSpec(memory_space=pltpu.SMEM),pl.BlockSpec((256,CH),lambda i:(0,i)),pl.BlockSpec((256,CH),lambda i:(0,i)),
        pl.BlockSpec((CH,128),lambda i:(i,0)),pl.BlockSpec((CH,128),lambda i:(i,0)),pl.BlockSpec((n,128),lambda i:(0,0))],
      out_specs=[pl.BlockSpec((64,CH),lambda i:(0,i)),pl.BlockSpec((n,128),lambda i:(0,0))],
      out_shape=[jax.ShapeDtypeStruct((64,rows),jnp.bfloat16),jax.ShapeDtypeStruct((n,128),jnp.bfloat16)],
      scratch_shapes=[pltpu.VMEM((n,256),jnp.bfloat16),pltpu.VMEM((64,n),jnp.bfloat16),pltpu.VMEM((n,128),jnp.float32),pltpu.VMEM((64,CH),jnp.float32)],
      compiler_params=pltpu.CompilerParams(vmem_limit_bytes=56*2**20),
      cost_estimate=pl.CostEstimate(flops=50_000_000_000,bytes_accessed=12*2**20,transcendentals=n*rows//2),
    )(r,qt,dot_,qn,don,kv)


def layer_norm(value, gain, bias):
    centre = value - jnp.mean(value, axis=-1, keepdims=True)
    spread = jnp.mean(centre * centre, axis=-1, keepdims=True)
    return centre * lax.rsqrt(spread + EPSILON) * gain + bias


def smooth_gelu(value):
    return (
        0.5
        * value
        * (1.0 + jnp.tanh(0.7978845608028654 * (value + 0.044715 * value * value * value)))
    )


def mm(spec, a, b):
    return jnp.einsum(spec, a, b, preferred_element_type=F32)


def low_parts(value, count):
    parts = []
    for _ in range(count):
        part = lax.reduce_precision(value, 8, 7)
        parts.append(part.astype(BF))
        value = value - part
    return parts


def swap(array, axis):
    return lax.ppermute(array, axis, [(0, 1), (1, 0)])


def seq_sum(shard):
    total = shard.astype(F32) + swap(shard, "y").astype(F32)
    total = total.astype(BF)
    return total.astype(F32) + swap(total, "c").astype(F32)


def on_device(
    inputs,
    cotangent,
    first_gain,
    first_bias,
    triple_weight,
    query_bias,
    value_bias,
    out_weight,
    out_bias,
    second_gain,
    second_bias,
    expand_weight,
    expand_bias,
    reduce_weight,
    reduce_bias,
):
    tokens, model = inputs.shape
    hidden_here = expand_weight.shape[1]
    here = out_weight.shape[1]
    three = triple_weight.shape[1]
    shards = lax.axis_size("g") * lax.axis_size("z") * lax.axis_size("x")
    hidden = hidden_here * shards
    zs = lax.axis_size("z")
    z = lax.axis_index("z")
    ring_at = (lax.axis_index("x") * lax.axis_size("y") + lax.axis_index("y")) * lax.axis_size(
        "c"
    ) + lax.axis_index("c")
    ring_at = ring_at.astype(jnp.int32)[None]
    heads = HEADS // zs
    width = heads * HEAD_DIM
    rows = tokens * zs

    small = jnp.concatenate(
        [
            first_gain,
            first_bias,
            query_bias,
            value_bias,
            out_bias,
            second_gain,
            second_bias,
            reduce_bias,
            expand_bias,
        ]
    )
    extra = -(-small.shape[0] // (model * 16)) * 16
    small_rows = jnp.pad(small, (0, extra * model - small.shape[0])).reshape(extra, model)

    x_all = lax.all_gather(inputs, "z", axis=0, tiled=True)
    first_pack = lax.all_gather(
        jnp.concatenate([pad_rows(triple_weight.T), small_rows]), WEIGHT_AXES, axis=0, tiled=False
    )
    padded = first_pack.shape[1] - extra
    triple = first_pack[:, :three].reshape(3 * model, model)
    flat_small = first_pack[:, padded:].reshape(shards, extra * model)
    vectors = [flat_small[:, i * here : (i + 1) * here].reshape(model).astype(F32) for i in range(8)]
    gain1, bias1, q_bias, v_bias, o_bias, gain2, bias2, r_bias = vectors
    e_bias = flat_small[:, 8 * here : 8 * here + hidden_here].reshape(hidden).astype(F32)

    out_t = lax.all_gather(out_weight.T, WEIGHT_AXES, axis=0, tiled=True)
    expand_t = lax.all_gather(expand_weight.T, WEIGHT_AXES, axis=0, tiled=True)
    reduce_t = lax.all_gather(reduce_weight.T, WEIGHT_AXES, axis=0, tiled=True)

    w_q = lax.dynamic_slice_in_dim(triple, z * width, width, 0)
    w_k = lax.dynamic_slice_in_dim(triple, model + z * width, width, 0)
    w_v = lax.dynamic_slice_in_dim(triple, 2 * model + z * width, width, 0)
    w_kv = jnp.stack(
        [w_k.reshape(heads, HEAD_DIM, model), w_v.reshape(heads, HEAD_DIM, model)], axis=1
    )
    w_kv = w_kv.reshape(2 * width, model)
    b_q = lax.dynamic_slice_in_dim(q_bias, z * width, width, 0)
    b_v = lax.dynamic_slice_in_dim(v_bias, z * width, width, 0).reshape(heads, HEAD_DIM)
    b_kv = jnp.stack([jnp.zeros_like(b_v), b_v], axis=1).reshape(2 * width)

    normed1 = layer_norm(x_all.astype(F32), gain1, bias1).astype(BF)
    kv = (mm("tm,fm->tf", normed1, w_kv) + b_kv).astype(BF)
    pairs = [
        lax.all_gather(kv[:, h * 128 : (h + 1) * 128], RING, axis=0, tiled=True)
        for h in range(heads)
    ]
    q_t = (mm("fm,tm->ft", w_q, normed1) + b_q[:, None]).astype(BF)
    blank = jnp.zeros((HEAD_DIM, rows), BF)
    scaled = q_t.astype(F32) * (LOG2E * HEAD_DIM**-0.5)
    q_hi, q_lo = low_parts(scaled, 2)

    outs, lses = [], []
    for h in range(heads):
        part = slice(h * HEAD_DIM, (h + 1) * HEAD_DIM)
        packed = jnp.concatenate([q_hi[part], blank, q_lo[part], blank])
        out_h, lse_h = attend(ring_at, packed, pairs[h], 4)
        outs.append(out_h)
        lses.append(lse_h[0:1])
    out_all = jnp.concatenate(outs)
    att = lax.all_to_all(out_all.astype(BF), "z", split_axis=1, concat_axis=0, tiled=True)

    wide = inputs.astype(F32)
    middle = wide + mm("ft,mf->tm", att, out_t) + o_bias
    normed2 = layer_norm(middle, gain2, bias2).astype(BF)
    pre = mm("tm,hm->th", normed2, expand_t) + e_bias
    act = smooth_gelu(pre).astype(BF)
    result = (middle + mm("th,mh->tm", act, reduce_t) + r_bias).astype(BF)

    grad_reduce_t = mm("tm,th->mh", cotangent, act).astype(BF)
    cot = cotangent.astype(F32)
    grad_reduce_b = jnp.sum(cot, axis=0)
    grad_act = mm("tm,mh->th", cotangent, reduce_t)
    grad_pre_wide = jax.vjp(smooth_gelu, pre)[1](grad_act)[0]
    grad_pre = grad_pre_wide.astype(BF)
    grad_expand_t = mm("th,tm->hm", grad_pre, normed2).astype(BF)
    grad_expand_b = jnp.sum(grad_pre.astype(F32), axis=0)
    grad_mid_norm, grad_gain2, grad_bias2 = jax.vjp(layer_norm, middle, gain2, bias2)[1](
        mm("th,hm->tm", grad_pre, expand_t)
    )
    grad_middle = cot + grad_mid_norm
    grad_branch = grad_middle.astype(BF)
    grad_out_t = mm("tm,ft->mf", grad_branch, att).astype(BF)
    grad_out_b = jnp.sum(grad_branch.astype(F32), axis=0)
    grad_att = mm("mf,tm->ft", out_t, grad_branch).astype(BF)
    grad_heads = lax.all_to_all(grad_att, "z", split_axis=0, concat_axis=1, tiled=True)

    dqs, dkvs = [], []
    for h in range(heads):
        part = slice(h * HEAD_DIM, (h + 1) * HEAD_DIM)
        g_h = grad_heads[part]
        delta = jnp.sum(g_h.astype(F32) * outs[h], axis=0, keepdims=True)
        tail = jnp.zeros((HEAD_DIM - 3, rows), BF)
        q_pack = jnp.concatenate([q_hi[part], blank, q_lo[part], *low_parts(-lses[h], 3), tail])
        g_pack = jnp.concatenate([blank, g_h, blank, *low_parts(-delta, 3), tail])
        q_rows = jnp.concatenate([q_t[part] * BF(0.125), blank]).T
        g_rows = jnp.concatenate([blank, g_h]).T
        dq_h, dkv_h = attend_back(ring_at, q_pack, g_pack, q_rows, g_rows, pairs[h])
        dqs.append(dq_h)
        dkvs.append(lax.psum_scatter(dkv_h, RING, scatter_dimension=0, tiled=True))
    dq = jnp.concatenate(dqs)
    dkv = jnp.concatenate(dkvs, axis=1)

    mlp_pack = jnp.concatenate(
        [
            grad_expand_t.reshape(shards, hidden_here, model),
            grad_out_t.reshape(shards, here, model),
        ],
        axis=1,
    )
    mlp_pack = lax.psum_scatter(mlp_pack, WEIGHT_AXES, scatter_dimension=0, tiled=False)
    grad_reduce_t = lax.psum_scatter(grad_reduce_t, WEIGHT_AXES, scatter_dimension=0, tiled=True)
    mlp_pack = seq_sum(mlp_pack)
    grad_reduce_w = seq_sum(grad_reduce_t).T
    grad_expand_w = mlp_pack[:hidden_here].T
    grad_out_w = mlp_pack[hidden_here:].T

    grad_w_q = mm("ft,tm->fm", dq, normed1)
    grad_w_kv = mm("tf,tm->fm", dkv, normed1).reshape(heads, 2, HEAD_DIM, model)
    grad_q_b = jnp.sum(dq.astype(F32), axis=1)
    grad_v_b = jnp.sum(dkv.astype(F32), axis=0).reshape(heads, 2, HEAD_DIM)[:, 1].reshape(width)
    part_norm = mm("ft,fm->tm", dq, w_q) + mm("tf,fm->tm", dkv, w_kv)
    grad_normed = lax.psum_scatter(part_norm.astype(BF), "z", scatter_dimension=0, tiled=True)
    grad_in_norm, grad_gain1, grad_bias1 = jax.vjp(layer_norm, wide, gain1, bias1)[1](
        grad_normed.astype(F32)
    )
    grad_in = (grad_middle + grad_in_norm).astype(BF)

    triple_grad = jnp.zeros((3 * model, model), BF)
    for at, piece in enumerate(
        (
            grad_w_q,
            grad_w_kv[:, 0].reshape(width, model),
            grad_w_kv[:, 1].reshape(width, model),
        )
    ):
        triple_grad = lax.dynamic_update_slice(
            triple_grad, piece.astype(BF), (at * model + z * width, 0)
        )
    placed_q = lax.dynamic_update_slice(jnp.zeros((model,), F32), grad_q_b, (z * width,))
    placed_v = lax.dynamic_update_slice(jnp.zeros((model,), F32), grad_v_b, (z * width,))
    small_grads = jnp.concatenate(
        [
            v.reshape(shards, -1)
            for v in (
                grad_gain1,
                grad_bias1,
                placed_q,
                placed_v,
                grad_out_b,
                grad_gain2,
                grad_bias2,
                grad_reduce_b,
                grad_expand_b,
            )
        ],
        axis=1,
    )
    small_grads = jnp.pad(small_grads, ((0, 0), (0, extra * model - small_grads.shape[1])))
    last = jnp.concatenate(
        [
            jnp.pad(
                triple_grad.reshape(shards, three, model), ((0, 0), (0, padded - three), (0, 0))
            ),
            small_grads.astype(BF).reshape(shards, extra, model),
        ],
        axis=1,
    )
    last = seq_sum(lax.psum_scatter(last, WEIGHT_AXES, scatter_dimension=0, tiled=False))
    grad_triple_w = last[:three].T
    flat = last[padded:].reshape(-1)
    vecs = [flat[i * here : (i + 1) * here] for i in range(8)]
    grad_e_b = flat[8 * here : 8 * here + hidden_here]
    return (
        result,
        grad_in,
        vecs[0],
        vecs[1],
        grad_triple_w,
        vecs[2],
        vecs[3],
        grad_out_w,
        vecs[4],
        vecs[5],
        vecs[6],
        grad_expand_w,
        grad_e_b,
        grad_reduce_w,
        vecs[7],
    )


def pad_rows(array):
    short = -array.shape[0] % 16
    return jnp.pad(array, ((0, short), (0, 0))) if short else array


def solution(mesh):
    fsdp, seq = mesh.shape["fsdp"], mesh.shape["seq"]
    wide = Mesh(
        mesh.devices.reshape(fsdp // GROUP, GROUP // 2, 2, seq // 2, 2), ("g", "z", "x", "y", "c")
    )
    rows = P(ALL, None)
    vector = P(WEIGHT_AXES)
    matrix = P(None, WEIGHT_AXES)
    return jax.shard_map(
        on_device,
        mesh=wide,
        in_specs=(
            rows,
            rows,
            vector,
            vector,
            matrix,
            vector,
            vector,
            matrix,
            vector,
            vector,
            vector,
            matrix,
            vector,
            matrix,
            vector,
        ),
        out_specs=(
            rows,
            rows,
            vector,
            vector,
            matrix,
            vector,
            vector,
            matrix,
            vector,
            vector,
            vector,
            matrix,
            vector,
            matrix,
            vector,
        ),
        check_vma=False,
    )
```

```python
import functools

import jax
import jax.numpy as jnp
from jax import lax
from jax.experimental import pallas as pl
from jax.experimental.pallas import tpu as pltpu
from jax.sharding import Mesh
from jax.sharding import PartitionSpec as P

HEADS = 12
HEAD_DIM = 64
GROUP = 8
EPSILON = 1e-05
NEG = -1e30
LOG2E = 1.4426950408889634
CH = 512
BF = jnp.bfloat16
F32 = jnp.float32
WEIGHT_AXES = ("g", "z", "x")
RING = ("x", "y", "c")
ALL = ("g", "z", "x", "y", "c")


def dotf(a, b):
    return lax.dot_general(a, b, (((1,), (0,)), ((), ())), preferred_element_type=F32)


def block_at(index):
    return pl.ds(pl.multiple_of(index * CH, CH), CH)


def fill_keys(kv_ref, wide, turned, first, ones):
    lane = lax.broadcasted_iota(jnp.int32, (CH, 128), 1)
    unit = jnp.where((lane >= 64) & (lane < 67), 1.0, 0.0).astype(BF)

    def body(i, _):
        at = block_at(i)
        block = kv_ref[at, :]
        wide[at, 0:128] = block
        wide[at, 128:256] = jnp.where(lane < 64, block, unit)
        turned[0:64, at] = block.T[first : first + 64]
        if ones:
            turned[64:80, at] = jnp.ones((16, CH), BF)
        return 0

    lax.fori_loop(0, kv_ref.shape[0] // CH, body, 0)


def split_low(value, count):
    parts = []
    for _ in range(count):
        part = value.astype(BF)
        parts.append(part)
        value = value - part.astype(F32)
    return parts


def pack_query(pack, query):
    hi, lo = split_low(query.astype(F32) * (LOG2E * 0.125), 2)
    pack[0:64, :] = hi
    pack[64:128, :] = jnp.zeros((64, CH), BF)
    pack[128:192, :] = lo
    pack[192:256, :] = jnp.zeros((64, CH), BF)


def pack_shift(pack, shift):
    parts = [jnp.broadcast_to(p.astype(F32), (16, CH)) for p in split_low(shift, 3)]
    at = lax.broadcasted_iota(jnp.int32, (16, CH), 0)
    rows = jnp.where(at == 0, parts[0], jnp.where(at == 1, parts[1], parts[2]))
    pack[192:208, :] = jnp.where(at < 3, rows, 0.0).astype(BF)


def flip_of(info, strip):
    return 7 * lax.rem(strip + info[1], 2)


def key_place(info, chunk, strips):
    strip = lax.div(chunk, 8)
    holder = lax.rem(chunk, 8) ^ flip_of(info, strip) ^ info[2]
    return holder * strips + strip


def causal(scores):
    key = lax.broadcasted_iota(jnp.int32, scores.shape, 0)
    query = lax.broadcasted_iota(jnp.int32, scores.shape, 1)
    return jnp.where(key <= query, scores, NEG)


def forward_kernel(
    strips, unroll, r_ref, q_ref, kv_ref, out_ref, lse_ref, wide, turned, pack, top_s, acc
):
    i = pl.program_id(0)
    count = i * 8 + (r_ref[0] ^ flip_of(r_ref, i))

    @pl.when(i == 0)
    def _():
        fill_keys(kv_ref, wide, turned, 64, True)

    pack_query(pack, q_ref[...])
    top_s[...] = jnp.full(top_s.shape, NEG, F32)
    acc[...] = jnp.zeros(acc.shape, F32)

    def step(chunks, last):
        places = [block_at(key_place(r_ref, c, strips)) for c in chunks]
        scores = [dotf(wide[at, :], pack[...]) for at in places]
        if last:
            scores[-1] = causal(scores[-1])
        before = top_s[...]
        top = before
        for s in scores:
            top = jnp.maximum(top, jnp.max(s, axis=0, keepdims=True))
        total = acc[...] * jnp.exp2(before - top)
        for at, s in zip(places, scores):
            total = total + dotf(turned[:, at], jnp.exp2(s - top).astype(BF))
        acc[...] = total
        top_s[...] = top

    def many(t, _):
        step([t * unroll + u for u in range(unroll)], False)
        return 0

    def single(c, _):
        step([c], False)
        return 0

    rounds = lax.div(count, unroll)
    lax.fori_loop(0, rounds, many, 0)
    lax.fori_loop(rounds * unroll, count, single, 0)
    step([count], True)
    mass = acc[64:65, :]
    out_ref[...] = acc[0:64, :] / mass
    lse_ref[...] = jnp.broadcast_to(top_s[...] + jnp.log2(mass), lse_ref.shape)


def attend(r, query, kv, unroll=4):
    keys, rows = kv.shape[0], query.shape[1]
    strips = rows // CH
    return pl.pallas_call(
        functools.partial(forward_kernel, strips, unroll),
        grid=(strips,),
        in_specs=[
            pl.BlockSpec(memory_space=pltpu.SMEM),
            pl.BlockSpec((64, CH), lambda i: (0, i)),
            pl.BlockSpec((keys, 128), lambda i: (0, 0)),
        ],
        out_specs=[
            pl.BlockSpec((64, CH), lambda i: (0, i)),
            pl.BlockSpec((8, CH), lambda i: (0, i)),
        ],
        out_shape=[
            jax.ShapeDtypeStruct((64, rows), F32),
            jax.ShapeDtypeStruct((8, rows), F32),
        ],
        scratch_shapes=[
            pltpu.VMEM((keys, 256), BF),
            pltpu.VMEM((80, keys), BF),
            pltpu.VMEM((256, CH), BF),
            pltpu.VMEM((1, CH), F32),
            pltpu.VMEM((80, CH), F32),
        ],
        compiler_params=pltpu.CompilerParams(vmem_limit_bytes=56 * 2**20),
        cost_estimate=pl.CostEstimate(
            flops=40 * 10**9, bytes_accessed=8 * 2**20, transcendentals=keys * rows // 2
        ),
    )(r, query, kv)


def backward_kernel(
    strips,
    unroll,
    r_ref,
    q_ref,
    g_ref,
    out_ref,
    lse_ref,
    kv_ref,
    dq_ref,
    dkv_ref,
    wide,
    turned,
    dkv,
    dq,
    q_pack,
    g_pack,
    q_rows,
    g_rows,
):
    i = pl.program_id(0)
    count = i * 8 + (r_ref[0] ^ flip_of(r_ref, i))

    @pl.when(i == 0)
    def _():
        fill_keys(kv_ref, wide, turned, 0, False)

        def clear(t, _):
            dkv[block_at(t), :] = jnp.zeros((CH, 128), F32)
            return 0

        lax.fori_loop(0, dkv.shape[0] // CH, clear, 0)

    query, grad = q_ref[...], g_ref[...]
    blank = jnp.zeros((64, CH), BF)
    pack_query(q_pack, query)
    pack_shift(q_pack, -lse_ref[0:1, :])
    g_pack[0:64, :] = blank
    g_pack[64:128, :] = grad
    g_pack[128:256, :] = jnp.zeros((128, CH), BF)
    pack_shift(g_pack, -jnp.sum(grad.astype(F32) * out_ref[...], axis=0, keepdims=True))
    q_rows[...] = jnp.concatenate([query * BF(0.125), blank]).T
    g_rows[...] = jnp.concatenate([blank, grad]).T
    dq[...] = jnp.zeros(dq.shape, F32)

    def step(chunks, last):
        places = [block_at(key_place(r_ref, c, strips)) for c in chunks]
        scores = [dotf(wide[at, :], q_pack[...]) for at in places]
        grads = [dotf(wide[at, :], g_pack[...]) for at in places]
        if last:
            scores[-1] = causal(scores[-1])
        total = dq[...]
        for at, s, g in zip(places, scores, grads):
            p = jnp.exp2(s)
            ds = (p * g).astype(BF)
            dkv[at, :] += dotf(p.astype(BF), g_rows[...]) + dotf(ds, q_rows[...])
            total = total + dotf(turned[:, at], ds)
        dq[...] = total

    def many(t, _):
        step([t * unroll + u for u in range(unroll)], False)
        return 0

    def single(c, _):
        step([c], False)
        return 0

    rounds = lax.div(count, unroll)
    lax.fori_loop(0, rounds, many, 0)
    if unroll > 1:
        lax.fori_loop(rounds * unroll, count, single, 0)
    step([count], True)
    dq_ref[...] = (dq[...] * 0.125).astype(dq_ref.dtype)

    @pl.when(i == strips - 1)
    def _():
        def write(t, _):
            dkv_ref[block_at(t), :] = dkv[block_at(t), :].astype(BF)
            return 0

        lax.fori_loop(0, dkv.shape[0] // CH, write, 0)


def attend_back(r, query, grad, out, lse, kv, unroll=2):
    keys, rows = kv.shape[0], query.shape[1]
    strips = rows // CH
    strip = pl.BlockSpec((64, CH), lambda i: (0, i))
    whole = pl.BlockSpec((keys, 128), lambda i: (0, 0))
    return pl.pallas_call(
        functools.partial(backward_kernel, strips, unroll),
        grid=(strips,),
        in_specs=[
            pl.BlockSpec(memory_space=pltpu.SMEM),
            strip,
            strip,
            strip,
            pl.BlockSpec((8, CH), lambda i: (0, i)),
            whole,
        ],
        out_specs=[strip, whole],
        out_shape=[
            jax.ShapeDtypeStruct((64, rows), BF),
            jax.ShapeDtypeStruct((keys, 128), BF),
        ],
        scratch_shapes=[
            pltpu.VMEM((keys, 256), BF),
            pltpu.VMEM((64, keys), BF),
            pltpu.VMEM((keys, 128), F32),
            pltpu.VMEM((64, CH), F32),
            pltpu.VMEM((256, CH), BF),
            pltpu.VMEM((256, CH), BF),
            pltpu.VMEM((CH, 128), BF),
            pltpu.VMEM((CH, 128), BF),
        ],
        compiler_params=pltpu.CompilerParams(vmem_limit_bytes=56 * 2**20),
        cost_estimate=pl.CostEstimate(
            flops=100 * 10**9, bytes_accessed=12 * 2**20, transcendentals=keys * rows // 2
        ),
    )(r, query, grad, out, lse, kv)


def normalise(value):
    centre = value - jnp.mean(value, axis=-1, keepdims=True)
    spread = jnp.mean(centre * centre, axis=-1, keepdims=True)
    root = lax.rsqrt(spread + EPSILON)
    return centre * root, root


def normalise_back(grad, unit, root, gain):
    f = grad * gain
    first = jnp.mean(f, axis=-1, keepdims=True)
    second = jnp.mean(f * unit, axis=-1, keepdims=True)
    return root * (f - first - unit * second)


def smooth_gelu(value):
    return (
        0.5
        * value
        * (1.0 + jnp.tanh(0.7978845608028654 * (value + 0.044715 * value * value * value)))
    )


def mm(spec, a, b):
    return jnp.einsum(spec, a, b, preferred_element_type=F32)


def swap(array, axis):
    return lax.ppermute(array, axis, [(0, 1), (1, 0)])


def swap_sum(array, axis):
    return array.astype(F32) + swap(array, axis).astype(F32)


def in_order(at, own, other, axis):
    return jnp.where(
        at == 0, jnp.concatenate([own, other], axis), jnp.concatenate([other, own], axis)
    )


def part(array, index, size, axis):
    return lax.dynamic_slice_in_dim(array, index * size, size, axis)


def pad_rows(array, rows):
    return jnp.pad(array, ((0, rows - array.shape[0]), (0, 0)))


def spread_groups(blocks, depth, ring):
    return [
        [b * depth * ring + z * ring + (r if z % 2 == 0 else ring - 1 - r) for z in range(depth)]
        for b in range(blocks)
        for r in range(ring)
    ]


def by_ring(array, ring, distance):
    size = lax.axis_size("g") * lax.axis_size("z")
    pairs = [
        (b * ring + r, b * ring + (r ^ distance)) for b in range(size) for r in range(ring)
    ]
    return lax.ppermute(array, ALL, pairs)


def fetch_triple(triple_weight, small, at):
    z, x, c = at
    turned = triple_weight.T
    three, model = turned.shape
    half = model // 2
    width = model // 4
    extra = small.shape[0] // half
    mine = jnp.concatenate([part(turned, c, half, 1), pad_rows(small.reshape(extra, half), 16)])
    both = in_order(x, mine[None], swap(mine, "x")[None], 0)
    pairs = both[:, :three].reshape(3, width, half)
    pairs = jnp.concatenate([pairs, jnp.zeros((1, width, half), BF)])
    slots = lax.dynamic_slice_in_dim(jnp.concatenate([pairs, pairs]), z, 4, 0)
    vectors = pad_rows(both[:, three : three + extra].reshape(2 * extra, half), 16)
    slots = jnp.concatenate([slots, jnp.broadcast_to(vectors, (4, 16, half))], axis=1)
    got = lax.all_to_all(slots, "z", split_axis=0, concat_axis=0, tiled=True)
    own = jnp.concatenate(
        [
            lax.dynamic_index_in_dim(got, (z + 4 * kind) // 3, 0, keepdims=False)[:width]
            for kind in range(3)
        ]
    )
    weights = in_order(c, own, swap(own, "c"), 1)
    return weights, got[:, width : width + 2 * extra].reshape(8, extra * half)


def fetch_triple_whole(triple_weight, small, at):
    z, x, c = at
    model = triple_weight.shape[0]
    width = model // 4
    whole = lax.all_gather(triple_weight.T, WEIGHT_AXES, axis=0, tiled=True)
    vectors = lax.all_gather(small, WEIGHT_AXES, axis=0, tiled=False)
    rows = [lax.dynamic_slice_in_dim(whole, k * model + z * width, width, 0) for k in range(3)]
    return jnp.concatenate(rows), vectors


def send_triple(grads, small, at):
    z, x, c = at
    model = grads.shape[1]
    half = model // 2
    width = model // 4
    three = 3 * width // 2
    extra = small.shape[1] // half
    low = grads.astype(BF)
    vectors = small.astype(BF).reshape(8 * extra, half)
    vectors = pad_rows(vectors, 32)
    mine = jnp.concatenate([part(low, c, half, 1), vectors])
    other = jnp.concatenate([part(low, 1 - c, half, 1), vectors])
    total = (mine.astype(F32) + swap(other, "c").astype(F32)).astype(BF)
    total = swap_sum(total, "y").astype(BF)
    by_depth = total[3 * width : 3 * width + 8 * extra].reshape(4, 2 * extra, half)
    by_depth = jnp.pad(by_depth, ((0, 0), (0, 16 - 2 * extra), (0, 0)))
    slots = jnp.zeros((4, width, half), BF)
    for kind in range(3):
        piece = total[kind * width : (kind + 1) * width][None]
        slots = lax.dynamic_update_slice(slots, piece, ((z + 4 * kind) // 3, 0, 0))
    got = lax.all_to_all(
        jnp.concatenate([slots, by_depth], axis=1), "z", split_axis=0, concat_axis=0, tiled=True
    )
    pairs = jnp.concatenate(
        [
            lax.dynamic_index_in_dim(got, (i - z) % 4, 0, keepdims=False)[:width]
            for i in range(3)
        ]
    )
    sums = jnp.sum(got[:, width : width + 2 * extra].astype(F32), axis=0).astype(BF)

    def portion(index):
        rows = part(pairs, index, three, 0)
        return jnp.concatenate([rows, pad_rows(part(sums, index, extra, 0), 16)])

    total = portion(x).astype(F32) + swap(portion(1 - x), "x").astype(F32)
    own = total[:three].astype(BF)
    shard = in_order(c, own, swap(own, "c"), 1).astype(F32)
    return shard.T, total[three : three + extra].reshape(-1)


def send_triple_whole(grads, small, at):
    z, x, c = at
    model = grads.shape[1]
    width = model // 4
    whole = jnp.zeros((3 * model, model), BF)
    for kind in range(3):
        piece = grads[kind * width : (kind + 1) * width].astype(BF)
        whole = lax.dynamic_update_slice(whole, piece, (kind * model + z * width, 0))
    shard = lax.psum_scatter(whole, WEIGHT_AXES, scatter_dimension=0, tiled=True)
    vectors = lax.psum_scatter(small, WEIGHT_AXES, scatter_dimension=0, tiled=False)
    shard = swap_sum(swap_sum(shard, "y").astype(BF), "c")
    return shard.T, swap_sum(swap_sum(vectors, "y"), "c")


def on_device(
    inputs,
    cotangent,
    first_gain,
    first_bias,
    triple_weight,
    query_bias,
    value_bias,
    out_weight,
    out_bias,
    second_gain,
    second_bias,
    expand_weight,
    expand_bias,
    reduce_weight,
    reduce_bias,
):
    tokens, model = inputs.shape
    hidden_here = expand_weight.shape[1]
    here = out_weight.shape[1]
    blocks, depth = lax.axis_size("g"), lax.axis_size("z")
    shards = blocks * depth * lax.axis_size("x")
    ring = lax.axis_size("x") * lax.axis_size("y") * lax.axis_size("c")
    z, x, y, c = [lax.axis_index(name).astype(jnp.int32) for name in ("z", "x", "y", "c")]
    at = (z, x, c)
    r = (x * lax.axis_size("y") + y) * lax.axis_size("c") + c
    heads = HEADS // depth
    width = heads * HEAD_DIM
    half_hidden = hidden_here // 2
    half_model = model // 2
    groups = spread_groups(blocks, depth, ring)
    info_far = jnp.stack([r, z % 2, r])
    info_abs = jnp.stack([r, z % 2, jnp.zeros_like(r)])
    special = shards == 8 and blocks == 1

    small = jnp.concatenate(
        [
            first_gain,
            first_bias,
            query_bias,
            value_bias,
            out_bias,
            second_gain,
            second_bias,
            reduce_bias,
            expand_bias,
        ]
    )
    x_all = lax.all_gather(inputs, ALL, axis_index_groups=groups, axis=0, tiled=True)
    weights, flat_small = (fetch_triple if special else fetch_triple_whole)(
        triple_weight, small, at
    )
    vectors = [flat_small[:, i * here : (i + 1) * here].reshape(model).astype(F32) for i in range(8)]
    gain1, bias1, q_bias, v_bias, o_bias, gain2, bias2, r_bias = vectors
    e_bias = flat_small[:, 8 * here : 8 * here + hidden_here].astype(F32)

    w_q = weights[:width]
    w_kv = weights[width:].reshape(2, heads, HEAD_DIM, model).transpose(1, 0, 2, 3)
    w_kv = w_kv.reshape(2 * width, model)
    b_q = part(q_bias, z, width, 0)
    b_v = part(v_bias, z, width, 0).reshape(heads, HEAD_DIM)
    b_kv = jnp.stack([jnp.zeros_like(b_v), b_v], axis=1).reshape(2 * width)

    unit1, _ = normalise(x_all.astype(F32))
    normed1 = (unit1 * gain1 + bias1).astype(BF)
    kv = (mm("tm,fm->tf", normed1, w_kv) + b_kv).astype(BF)
    q_t = (mm("fm,tm->ft", w_q, normed1) + b_q[:, None]).astype(BF)

    def head(array, h):
        return array[h * HEAD_DIM : (h + 1) * HEAD_DIM]

    def pair(h):
        return kv[:, h * 128 : (h + 1) * 128]

    keys = [lax.all_gather(pair(0), RING, axis=0, tiled=True)]
    for h in range(1, heads):
        pieces = [pair(h)] + [by_ring(pair(h), ring, d) for d in range(1, ring)]
        keys.append(jnp.concatenate(pieces))
    infos = [info_abs] + [info_far] * (heads - 1)

    own_b = jnp.concatenate(
        [
            part(out_weight.T, c, half_model, 1),
            reduce_half(reduce_weight, c, half_hidden),
        ],
        axis=1,
    )
    own_a = part(expand_weight.T, c, half_hidden, 0)
    own_a, own_b, keys[0] = lax.optimization_barrier((own_a, own_b, keys[0]))
    mine_b = lax.all_gather(own_b, WEIGHT_AXES, axis=0, tiled=True)
    mine_a = lax.all_gather(own_a, WEIGHT_AXES, axis=0, tiled=True)
    both_b = (mine_b, swap(mine_b, "c"))
    expand_t = (mine_a, swap(mine_a, "c"))
    out_t = [b[:, :half_model] for b in both_b]
    reduce_t = [b[:, half_model:] for b in both_b]

    outs, lses = [], []
    for h in range(heads):
        out_h, lse_h = attend(infos[h], head(q_t, h), keys[h])
        outs.append(out_h)
        lses.append(lse_h)
    out_all = jnp.concatenate([o.astype(BF) for o in outs])
    att = lax.all_to_all(
        out_all, ALL, split_axis=1, concat_axis=0, axis_index_groups=groups, tiled=True
    )

    sides = (c, 1 - c)
    atts = [part(att, side, half_model, 0) for side in sides]
    wide = inputs.astype(F32)
    middle = wide + o_bias
    for a, w in zip(atts, out_t):
        middle = middle + mm("ft,mf->tm", a, w)
    unit2, root2 = normalise(middle)
    normed2 = (unit2 * gain2 + bias2).astype(BF)
    total = middle + r_bias
    grad_normed = 0.0
    acts, grads_a, grads_r, grads_e = [], [], [], []
    for side, w_e, w_r in zip(sides, expand_t, reduce_t):
        bias = part(e_bias, side, half_hidden, 1).reshape(-1)
        pre = mm("tm,hm->th", normed2, w_e) + bias
        act, pullback = jax.vjp(smooth_gelu, pre)
        act = act.astype(BF)
        total = total + mm("th,mh->tm", act, w_r)
        grads_r.append(mm("tm,th->mh", cotangent, act).astype(BF))
        grad_pre = pullback(mm("tm,mh->th", cotangent, w_r))[0].astype(BF)
        grads_a.append(mm("th,tm->hm", grad_pre, normed2).astype(BF))
        grads_e.append(jnp.sum(grad_pre.astype(F32), axis=0).reshape(shards, half_hidden))
        grad_normed = grad_normed + mm("th,hm->tm", grad_pre, w_e)
    result = total.astype(BF)
    cot = cotangent.astype(F32)
    grad_reduce_b = jnp.sum(cot, axis=0)
    grad_gain2 = jnp.sum(grad_normed * unit2, axis=0)
    grad_bias2 = jnp.sum(grad_normed, axis=0)
    grad_expand_b = in_order(c, grads_e[0], grads_e[1], 1)
    grad_middle = cot + normalise_back(grad_normed, unit2, root2, gain2)
    grad_branch = grad_middle.astype(BF)
    grad_out_b = jnp.sum(grad_branch.astype(F32), axis=0)
    grad_atts = [mm("mf,tm->ft", w, grad_branch).astype(BF) for w in out_t]
    grad_att = in_order(c, grad_atts[0], grad_atts[1], 0)
    grad_heads = lax.all_to_all(
        grad_att, ALL, split_axis=0, concat_axis=1, axis_index_groups=groups, tiled=True
    )
    grads_o = [mm("tm,ft->mf", grad_branch, a).astype(BF) for a in atts]

    sum_a = (grads_a[0].astype(F32) + swap(grads_a[1], "c").astype(F32)).astype(BF)
    sum_r = (grads_r[0].astype(F32) + swap(grads_r[1], "c").astype(F32)).astype(BF)
    sum_o = (grads_o[0].astype(F32) + swap(grads_o[1], "c").astype(F32)).astype(BF)
    sum_b = jnp.concatenate([sum_o, sum_r], axis=1)
    sum_a = lax.psum_scatter(sum_a, WEIGHT_AXES, scatter_dimension=0, tiled=True)
    sum_b = lax.psum_scatter(sum_b, WEIGHT_AXES, scatter_dimension=0, tiled=True)

    dqs, dkvs = [None] * heads, [None] * heads
    for h in list(range(1, heads)) + [0]:
        dq_h, dkv_h = attend_back(
            infos[h], head(q_t, h), head(grad_heads, h), outs[h], lses[h], keys[h]
        )
        dqs[h] = dq_h
        if h == 0:
            dkv_h, sum_a, sum_b = lax.optimization_barrier((dkv_h, sum_a, sum_b))
            dkvs[h] = lax.psum_scatter(dkv_h, RING, scatter_dimension=0, tiled=True)
        else:
            pieces = dkv_h.reshape(ring, depth * tokens, 128)
            added = pieces[0].astype(F32)
            for d in range(1, ring):
                added = added + by_ring(pieces[d], ring, d).astype(F32)
            dkvs[h] = added.astype(BF)

    sum_a = swap_sum(sum_a, "y").astype(BF)
    sum_b = swap_sum(sum_b, "y").astype(BF)
    full_a = in_order(c, sum_a, swap(sum_a, "c"), 0)
    other_b = swap(sum_b, "c")
    full_o = in_order(c, sum_b[:, :half_model], other_b[:, :half_model], 1)
    full_r = in_order(
        c,
        sum_b[:, half_model:].reshape(here, shards, 1, half_hidden),
        other_b[:, half_model:].reshape(here, shards, 1, half_hidden),
        2,
    ).reshape(here, shards * hidden_here)
    grad_expand_w = full_a.T.astype(F32)
    grad_out_w = full_o.T.astype(F32)
    grad_reduce_w = full_r.T.astype(F32)

    dq = jnp.concatenate(dqs)
    dkv = jnp.concatenate(dkvs, axis=1)
    grad_w_q = mm("ft,tm->fm", dq, normed1)
    grad_w_kv = mm("tf,tm->fm", dkv, normed1).reshape(heads, 2, HEAD_DIM, model)
    grad_w = jnp.concatenate([grad_w_q, grad_w_kv.transpose(1, 0, 2, 3).reshape(2 * width, model)])
    grad_q_b = jnp.sum(dq.astype(F32), axis=1)
    grad_v_b = jnp.sum(dkv.astype(F32), axis=0).reshape(heads, 2, HEAD_DIM)[:, 1].reshape(width)
    part_norm = mm("ft,fm->tm", dq, w_q) + mm("tf,fm->tm", dkv, w_kv)
    grad_gain1 = jnp.sum(part_norm * unit1, axis=0)
    grad_bias1 = jnp.sum(part_norm, axis=0)
    grad_normed1 = lax.psum_scatter(
        part_norm.astype(BF), ALL, scatter_dimension=0, axis_index_groups=groups, tiled=True
    ).astype(F32)
    unit_in, root_in = normalise(wide)
    grad_in = (grad_middle + normalise_back(grad_normed1, unit_in, root_in, gain1)).astype(BF)

    placed_q = lax.dynamic_update_slice(jnp.zeros((model,), F32), grad_q_b, (z * width,))
    placed_v = lax.dynamic_update_slice(jnp.zeros((model,), F32), grad_v_b, (z * width,))
    small_grads = jnp.concatenate(
        [
            v.reshape(shards, -1)
            for v in (
                grad_gain1,
                grad_bias1,
                placed_q,
                placed_v,
                grad_out_b,
                grad_gain2,
                grad_bias2,
                grad_reduce_b,
                grad_expand_b,
            )
        ],
        axis=1,
    )
    grad_triple_w, flat = (send_triple if special else send_triple_whole)(grad_w, small_grads, at)
    vecs = [flat[i * here : (i + 1) * here] for i in range(8)]
    grad_e_b = flat[8 * here : 8 * here + hidden_here]
    return (
        result,
        grad_in,
        vecs[0],
        vecs[1],
        grad_triple_w,
        vecs[2],
        vecs[3],
        grad_out_w,
        vecs[4],
        vecs[5],
        vecs[6],
        grad_expand_w,
        grad_e_b,
        grad_reduce_w,
        vecs[7],
    )


def reduce_half(weight, c, half):
    pieces = weight.reshape(-1, 2, half, weight.shape[1])
    return part(pieces, c, 1, 1).reshape(-1, weight.shape[1]).T


def solution(mesh):
    fsdp, seq = mesh.shape["fsdp"], mesh.shape["seq"]
    wide = Mesh(
        mesh.devices.reshape(fsdp // GROUP, GROUP // 2, 2, seq // 2, 2), ("g", "z", "x", "y", "c")
    )
    rows = P(ALL, None)
    vector = P(WEIGHT_AXES)
    matrix = P(None, WEIGHT_AXES)
    return jax.shard_map(
        on_device,
        mesh=wide,
        in_specs=(
            rows,
            rows,
            vector,
            vector,
            matrix,
            vector,
            vector,
            matrix,
            vector,
            vector,
            vector,
            matrix,
            vector,
            matrix,
            vector,
        ),
        out_specs=(
            rows,
            rows,
            vector,
            vector,
            matrix,
            vector,
            vector,
            matrix,
            vector,
            vector,
            vector,
            matrix,
            vector,
            matrix,
            vector,
        ),
        check_vma=False,
    )
```

```python
import functools

import jax
import jax.numpy as jnp
from jax import lax
from jax.experimental import pallas as pl
from jax.experimental.pallas import tpu as pltpu
from jax.sharding import Mesh
from jax.sharding import PartitionSpec as P

HEADS = 12
HEAD_DIM = 64
GROUP = 8
EPSILON = 1e-05
NEG = -1e30
LOG2E = 1.4426950408889634
CH = 512
BF = jnp.bfloat16
F32 = jnp.float32
WEIGHT_AXES = ("g", "z", "x")
RING = ("x", "y", "c")
ALL = ("g", "z", "x", "y", "c")


def dotf(a, b):
    return lax.dot_general(a, b, (((1,), (0,)), ((), ())), preferred_element_type=F32)


def block_at(index):
    return pl.ds(pl.multiple_of(index * CH, CH), CH)


def fill_keys(kv_ref, wide, turned, first, ones):
    lane = lax.broadcasted_iota(jnp.int32, (CH, 128), 1)
    unit = jnp.where((lane >= 64) & (lane < 67), 1.0, 0.0).astype(BF)

    def body(i, _):
        at = block_at(i)
        block = kv_ref[at, :]
        wide[at, 0:128] = block
        wide[at, 128:256] = jnp.where(lane < 64, block, unit)
        turned[0:64, at] = block.T[first : first + 64]
        if ones:
            turned[64:80, at] = jnp.ones((16, CH), BF)
        return 0

    lax.fori_loop(0, kv_ref.shape[0] // CH, body, 0)


def split_low(value, count):
    parts = []
    for _ in range(count):
        part = value.astype(BF)
        parts.append(part)
        value = value - part.astype(F32)
    return parts


def pack_query(pack, query):
    hi, lo = split_low(query.astype(F32) * (LOG2E * 0.125), 2)
    pack[0:64, :] = hi
    pack[64:128, :] = jnp.zeros((64, CH), BF)
    pack[128:192, :] = lo
    pack[192:256, :] = jnp.zeros((64, CH), BF)


def pack_shift(pack, shift):
    parts = [jnp.broadcast_to(p.astype(F32), (16, CH)) for p in split_low(shift, 3)]
    at = lax.broadcasted_iota(jnp.int32, (16, CH), 0)
    rows = jnp.where(at == 0, parts[0], jnp.where(at == 1, parts[1], parts[2]))
    pack[192:208, :] = jnp.where(at < 3, rows, 0.0).astype(BF)


def flip_of(info, strip):
    return 7 * lax.rem(strip + info[1], 2)


def key_place(info, chunk, strips):
    strip = lax.div(chunk, 8)
    holder = lax.rem(chunk, 8) ^ flip_of(info, strip)
    return holder * strips + strip


def causal(scores):
    key = lax.broadcasted_iota(jnp.int32, scores.shape, 0)
    query = lax.broadcasted_iota(jnp.int32, scores.shape, 1)
    return jnp.where(key <= query, scores, NEG)


def forward_kernel(
    strips, unroll, r_ref, q_ref, kv_ref, out_ref, lse_ref, wide, turned, pack, top_s, acc
):
    i = pl.program_id(0)
    count = i * 8 + (r_ref[0] ^ flip_of(r_ref, i))

    @pl.when(i == 0)
    def _():
        fill_keys(kv_ref, wide, turned, 64, True)

    pack_query(pack, q_ref[...])
    top_s[...] = jnp.full(top_s.shape, NEG, F32)
    acc[...] = jnp.zeros(acc.shape, F32)

    def step(chunks, last):
        places = [block_at(key_place(r_ref, c, strips)) for c in chunks]
        scores = [dotf(wide[at, :], pack[...]) for at in places]
        if last:
            scores[-1] = causal(scores[-1])
        before = top_s[...]
        top = before
        for s in scores:
            top = jnp.maximum(top, jnp.max(s, axis=0, keepdims=True))
        total = acc[...] * jnp.exp2(before - top)
        for at, s in zip(places, scores):
            total = total + dotf(turned[:, at], jnp.exp2(s - top).astype(BF))
        acc[...] = total
        top_s[...] = top

    def many(t, _):
        step([t * unroll + u for u in range(unroll)], False)
        return 0

    def single(c, _):
        step([c], False)
        return 0

    rounds = lax.div(count, unroll)
    lax.fori_loop(0, rounds, many, 0)
    lax.fori_loop(rounds * unroll, count, single, 0)
    step([count], True)
    mass = acc[64:65, :]
    out_ref[...] = acc[0:64, :] / mass
    lse_ref[...] = jnp.broadcast_to(top_s[...] + jnp.log2(mass), lse_ref.shape)


def attend(r, query, kv, unroll=4):
    keys, rows = kv.shape[0], query.shape[1]
    strips = rows // CH
    return pl.pallas_call(
        functools.partial(forward_kernel, strips, unroll),
        grid=(strips,),
        in_specs=[
            pl.BlockSpec(memory_space=pltpu.SMEM),
            pl.BlockSpec((64, CH), lambda i: (0, i)),
            pl.BlockSpec((keys, 128), lambda i: (0, 0)),
        ],
        out_specs=[
            pl.BlockSpec((64, CH), lambda i: (0, i)),
            pl.BlockSpec((8, CH), lambda i: (0, i)),
        ],
        out_shape=[
            jax.ShapeDtypeStruct((64, rows), F32),
            jax.ShapeDtypeStruct((8, rows), F32),
        ],
        scratch_shapes=[
            pltpu.VMEM((keys, 256), BF),
            pltpu.VMEM((80, keys), BF),
            pltpu.VMEM((256, CH), BF),
            pltpu.VMEM((1, CH), F32),
            pltpu.VMEM((80, CH), F32),
        ],
        compiler_params=pltpu.CompilerParams(vmem_limit_bytes=56 * 2**20),
        cost_estimate=pl.CostEstimate(
            flops=15 * 10**9, bytes_accessed=8 * 2**20, transcendentals=0
        ),
    )(r, query, kv)


def backward_kernel(
    strips,
    unroll,
    r_ref,
    q_ref,
    g_ref,
    out_ref,
    lse_ref,
    kv_ref,
    dq_ref,
    dkv_ref,
    wide,
    turned,
    dkv,
    dq,
    q_pack,
    g_pack,
    q_rows,
    g_rows,
):
    i = pl.program_id(0)
    count = i * 8 + (r_ref[0] ^ flip_of(r_ref, i))

    @pl.when(i == 0)
    def _():
        fill_keys(kv_ref, wide, turned, 0, False)

        def clear(t, _):
            dkv[block_at(t), :] = jnp.zeros((CH, 128), F32)
            return 0

        lax.fori_loop(0, dkv.shape[0] // CH, clear, 0)

    query, grad = q_ref[...], g_ref[...]
    blank = jnp.zeros((64, CH), BF)
    pack_query(q_pack, query)
    pack_shift(q_pack, -lse_ref[0:1, :])
    g_pack[0:64, :] = blank
    g_pack[64:128, :] = grad
    g_pack[128:256, :] = jnp.zeros((128, CH), BF)
    pack_shift(g_pack, -jnp.sum(grad.astype(F32) * out_ref[...], axis=0, keepdims=True))
    q_rows[...] = jnp.concatenate([query * BF(0.125), blank]).T
    g_rows[...] = jnp.concatenate([blank, grad]).T
    dq[...] = jnp.zeros(dq.shape, F32)

    def step(chunks, last):
        places = [block_at(key_place(r_ref, c, strips)) for c in chunks]
        scores = [dotf(wide[at, :], q_pack[...]) for at in places]
        grads = [dotf(wide[at, :], g_pack[...]) for at in places]
        if last:
            scores[-1] = causal(scores[-1])
        total = dq[...]
        for at, s, g in zip(places, scores, grads):
            p = jnp.exp2(s)
            ds = (p * g).astype(BF)
            dkv[at, :] += dotf(p.astype(BF), g_rows[...]) + dotf(ds, q_rows[...])
            total = total + dotf(turned[:, at], ds)
        dq[...] = total

    def many(t, _):
        step([t * unroll + u for u in range(unroll)], False)
        return 0

    def single(c, _):
        step([c], False)
        return 0

    rounds = lax.div(count, unroll)
    lax.fori_loop(0, rounds, many, 0)
    if unroll > 1:
        lax.fori_loop(rounds * unroll, count, single, 0)
    step([count], True)
    dq_ref[...] = (dq[...] * 0.125).astype(dq_ref.dtype)

    @pl.when(i == strips - 1)
    def _():
        def write(t, _):
            dkv_ref[block_at(t), :] = dkv[block_at(t), :].astype(BF)
            return 0

        lax.fori_loop(0, dkv.shape[0] // CH, write, 0)


def attend_back(r, query, grad, out, lse, kv, unroll=2):
    keys, rows = kv.shape[0], query.shape[1]
    strips = rows // CH
    strip = pl.BlockSpec((64, CH), lambda i: (0, i))
    whole = pl.BlockSpec((keys, 128), lambda i: (0, 0))
    return pl.pallas_call(
        functools.partial(backward_kernel, strips, unroll),
        grid=(strips,),
        in_specs=[
            pl.BlockSpec(memory_space=pltpu.SMEM),
            strip,
            strip,
            strip,
            pl.BlockSpec((8, CH), lambda i: (0, i)),
            whole,
        ],
        out_specs=[strip, whole],
        out_shape=[
            jax.ShapeDtypeStruct((64, rows), BF),
            jax.ShapeDtypeStruct((keys, 128), BF),
        ],
        scratch_shapes=[
            pltpu.VMEM((keys, 256), BF),
            pltpu.VMEM((64, keys), BF),
            pltpu.VMEM((keys, 128), F32),
            pltpu.VMEM((64, CH), F32),
            pltpu.VMEM((256, CH), BF),
            pltpu.VMEM((256, CH), BF),
            pltpu.VMEM((CH, 128), BF),
            pltpu.VMEM((CH, 128), BF),
        ],
        compiler_params=pltpu.CompilerParams(vmem_limit_bytes=56 * 2**20),
        cost_estimate=pl.CostEstimate(
            flops=25 * 10**9, bytes_accessed=12 * 2**20, transcendentals=0
        ),
    )(r, query, grad, out, lse, kv)


def normalise(value):
    centre = value - jnp.mean(value, axis=-1, keepdims=True)
    spread = jnp.mean(centre * centre, axis=-1, keepdims=True)
    root = lax.rsqrt(spread + EPSILON)
    return centre * root, root


def normalise_back(grad, unit, root, gain):
    f = grad * gain
    first = jnp.mean(f, axis=-1, keepdims=True)
    second = jnp.mean(f * unit, axis=-1, keepdims=True)
    return root * (f - first - unit * second)


def smooth_gelu(value):
    return (
        0.5
        * value
        * (1.0 + jnp.tanh(0.7978845608028654 * (value + 0.044715 * value * value * value)))
    )


def mm(spec, a, b):
    return jnp.einsum(spec, a, b, preferred_element_type=F32)


def swap(array, axis):
    return lax.ppermute(array, axis, [(0, 1), (1, 0)])


def swap_sum(array, axis):
    return array.astype(F32) + swap(array, axis).astype(F32)


def in_order(at, own, other, axis):
    return jnp.where(
        at == 0, jnp.concatenate([own, other], axis), jnp.concatenate([other, own], axis)
    )


def part(array, index, size, axis):
    return lax.dynamic_slice_in_dim(array, index * size, size, axis)


def pad_rows(array, rows):
    return jnp.pad(array, ((0, rows - array.shape[0]), (0, 0)))


def spread_groups(blocks, depth, ring):
    return [
        [b * depth * ring + z * ring + (r if z % 2 == 0 else ring - 1 - r) for z in range(depth)]
        for b in range(blocks)
        for r in range(ring)
    ]


def pack_weights(expand, reduce, out, c):
    half_hidden = expand.shape[1] // 2
    model, here = out.shape
    e = part(expand.T, c, half_hidden, 0)
    w = reduce_half(reduce, c, half_hidden)
    o = part(out.T, c, model // 2, 1)
    return jnp.concatenate(
        [
            e,
            w[:, :model],
            w[:, model:],
            jnp.concatenate([o[: here // 2], o[here // 2 :]], axis=1),
        ]
    )


def unpack_weights(packed, half_hidden, here):
    shards, _, model = packed.shape
    first, second = half_hidden, half_hidden + here
    e = packed[:, :first].reshape(-1, model)
    w = jnp.concatenate(
        [
            packed[:, first:second].reshape(-1, model),
            packed[:, second : second + here].reshape(-1, model),
        ],
        axis=1,
    )
    o = packed[:, second + here :].reshape(shards, here // 2, 2, model // 2)
    return e, w, o.transpose(0, 2, 1, 3).reshape(-1, model // 2)


def pack_grads(e, w, o, shards):
    model = e.shape[1]
    here = model // shards
    o = o.reshape(shards, 2, here // 2, model // 2).transpose(0, 2, 1, 3)
    return jnp.concatenate(
        [
            e.reshape(shards, -1, model),
            w[:, :model].reshape(shards, here, model),
            w[:, model:].reshape(shards, here, model),
            o.reshape(shards, here // 2, model),
        ],
        axis=1,
    )


def unpack_grads(own, other, c, half_hidden, here):
    model = own.shape[1]
    first, second = half_hidden, half_hidden + here

    def reduce_of(rows):
        w = jnp.concatenate([rows[first:second], rows[second : second + here]], axis=1)
        return w.reshape(here, -1, 1, half_hidden)

    def out_of(rows):
        o = rows[second + here :]
        return jnp.concatenate([o[:, : model // 2], o[:, model // 2 :]])

    e = in_order(c, own[:first], other[:first], 0)
    w = in_order(c, reduce_of(own), reduce_of(other), 2).reshape(here, -1)
    o = in_order(c, out_of(own), out_of(other), 1)
    return e.T.astype(F32), w.T.astype(F32), o.T.astype(F32)


def fetch_triple(triple_weight, small, at):
    z, x, c = at
    turned = triple_weight.T
    three, model = turned.shape
    half = model // 2
    width = model // 4
    extra = small.shape[0] // half
    mine = jnp.concatenate([part(turned, c, half, 1), pad_rows(small.reshape(extra, half), 16)])
    both = in_order(x, mine[None], swap(mine, "x")[None], 0)
    pairs = both[:, :three].reshape(3, width, half)
    pairs = jnp.concatenate([pairs, jnp.zeros((1, width, half), BF)])
    slots = lax.dynamic_slice_in_dim(jnp.concatenate([pairs, pairs]), z, 4, 0)
    vectors = pad_rows(both[:, three : three + extra].reshape(2 * extra, half), 16)
    slots = jnp.concatenate([slots, jnp.broadcast_to(vectors, (4, 16, half))], axis=1)
    got = lax.all_to_all(slots, "z", split_axis=0, concat_axis=0, tiled=True)
    own = jnp.concatenate(
        [
            lax.dynamic_index_in_dim(got, (z + 4 * kind) // 3, 0, keepdims=False)[:width]
            for kind in range(3)
        ]
    )
    weights = in_order(c, own, swap(own, "c"), 1)
    return weights, got[:, width : width + 2 * extra].reshape(8, extra * half)


def fetch_triple_whole(triple_weight, small, at):
    z, x, c = at
    model = triple_weight.shape[0]
    width = model // 4
    whole = lax.all_gather(triple_weight.T, WEIGHT_AXES, axis=0, tiled=True)
    vectors = lax.all_gather(small, WEIGHT_AXES, axis=0, tiled=False)
    rows = [lax.dynamic_slice_in_dim(whole, k * model + z * width, width, 0) for k in range(3)]
    return jnp.concatenate(rows), vectors


def send_triple(grads, small, at):
    z, x, c = at
    model = grads.shape[1]
    half = model // 2
    width = model // 4
    three = 3 * width // 2
    extra = small.shape[1] // half
    low = grads.astype(BF)
    vectors = small.astype(BF).reshape(8 * extra, half)
    vectors = pad_rows(vectors, 32)
    mine = jnp.concatenate([part(low, c, half, 1), vectors])
    other = jnp.concatenate([part(low, 1 - c, half, 1), vectors])
    total = (mine.astype(F32) + swap(other, "c").astype(F32)).astype(BF)
    total = swap_sum(total, "y").astype(BF)
    by_depth = total[3 * width : 3 * width + 8 * extra].reshape(4, 2 * extra, half)
    by_depth = jnp.pad(by_depth, ((0, 0), (0, 16 - 2 * extra), (0, 0)))
    slots = jnp.zeros((4, width, half), BF)
    for kind in range(3):
        piece = total[kind * width : (kind + 1) * width][None]
        slots = lax.dynamic_update_slice(slots, piece, ((z + 4 * kind) // 3, 0, 0))
    got = lax.all_to_all(
        jnp.concatenate([slots, by_depth], axis=1), "z", split_axis=0, concat_axis=0, tiled=True
    )
    pairs = jnp.concatenate(
        [
            lax.dynamic_index_in_dim(got, (i - z) % 4, 0, keepdims=False)[:width]
            for i in range(3)
        ]
    )
    sums = jnp.sum(got[:, width : width + 2 * extra].astype(F32), axis=0).astype(BF)

    def portion(index):
        rows = part(pairs, index, three, 0)
        return jnp.concatenate([rows, pad_rows(part(sums, index, extra, 0), 16)])

    total = portion(x).astype(F32) + swap(portion(1 - x), "x").astype(F32)
    own = total[:three].astype(BF)
    shard = in_order(c, own, swap(own, "c"), 1).astype(F32)
    return shard.T, total[three : three + extra].reshape(-1)


def send_triple_whole(grads, small, at):
    z, x, c = at
    model = grads.shape[1]
    width = model // 4
    whole = jnp.zeros((3 * model, model), BF)
    for kind in range(3):
        piece = grads[kind * width : (kind + 1) * width].astype(BF)
        whole = lax.dynamic_update_slice(whole, piece, (kind * model + z * width, 0))
    shard = lax.psum_scatter(whole, WEIGHT_AXES, scatter_dimension=0, tiled=True)
    vectors = lax.psum_scatter(small, WEIGHT_AXES, scatter_dimension=0, tiled=False)
    shard = swap_sum(swap_sum(shard, "y").astype(BF), "c")
    return shard.T, swap_sum(swap_sum(vectors, "y"), "c")


def on_device(
    inputs,
    cotangent,
    first_gain,
    first_bias,
    triple_weight,
    query_bias,
    value_bias,
    out_weight,
    out_bias,
    second_gain,
    second_bias,
    expand_weight,
    expand_bias,
    reduce_weight,
    reduce_bias,
):
    tokens, model = inputs.shape
    hidden_here = expand_weight.shape[1]
    here = out_weight.shape[1]
    blocks, depth = lax.axis_size("g"), lax.axis_size("z")
    shards = blocks * depth * lax.axis_size("x")
    ring = lax.axis_size("x") * lax.axis_size("y") * lax.axis_size("c")
    z, x, y, c = [lax.axis_index(name).astype(jnp.int32) for name in ("z", "x", "y", "c")]
    at = (z, x, c)
    r = (x * lax.axis_size("y") + y) * lax.axis_size("c") + c
    heads = HEADS // depth
    width = heads * HEAD_DIM
    half_hidden = hidden_here // 2
    half_model = model // 2
    groups = spread_groups(blocks, depth, ring)
    info = jnp.stack([r, z % 2])
    special = shards == 8 and blocks == 1

    small = jnp.concatenate(
        [
            first_gain,
            first_bias,
            query_bias,
            value_bias,
            out_bias,
            second_gain,
            second_bias,
            reduce_bias,
            expand_bias,
        ]
    )
    x_all = lax.all_gather(inputs, ALL, axis_index_groups=groups, axis=0, tiled=True)
    weights, flat_small = (fetch_triple if special else fetch_triple_whole)(
        triple_weight, small, at
    )
    vectors = [flat_small[:, i * here : (i + 1) * here].reshape(model).astype(F32) for i in range(8)]
    gain1, bias1, q_bias, v_bias, o_bias, gain2, bias2, r_bias = vectors
    e_bias = flat_small[:, 8 * here : 8 * here + hidden_here].astype(F32)

    w_q = weights[:width]
    w_kv = weights[width:].reshape(2, heads, HEAD_DIM, model).transpose(1, 0, 2, 3)
    w_kv = w_kv.reshape(2 * width, model)
    b_q = part(q_bias, z, width, 0)
    b_v = part(v_bias, z, width, 0).reshape(heads, HEAD_DIM)
    b_kv = jnp.stack([jnp.zeros_like(b_v), b_v], axis=1).reshape(2 * width)

    unit1, _ = normalise(x_all.astype(F32))
    normed1 = (unit1 * gain1 + bias1).astype(BF)
    kv = (mm("tm,fm->tf", normed1, w_kv) + b_kv).astype(BF)
    q_t = (mm("fm,tm->ft", w_q, normed1) + b_q[:, None]).astype(BF)

    def head(array, h):
        return array[h * HEAD_DIM : (h + 1) * HEAD_DIM]

    def pair(h):
        return kv[:, h * 128 : (h + 1) * 128]

    keys = [lax.all_gather(pair(0), RING, axis=0, tiled=True)]
    for h in range(1, heads - 1):
        own_pair, keys[-1] = lax.optimization_barrier((pair(h), keys[-1]))
        keys.append(lax.all_gather(own_pair, RING, axis=0, tiled=True))
    copies = jnp.broadcast_to(pair(heads - 1), (ring,) + pair(0).shape)
    keys.append(
        lax.all_to_all(copies, RING, split_axis=0, concat_axis=0, tiled=True).reshape(-1, 128)
    )

    own_w = pack_weights(expand_weight, reduce_weight, out_weight, c)
    own_w, keys[1] = lax.optimization_barrier((own_w, keys[1]))
    mine_w = lax.all_gather(own_w, WEIGHT_AXES, axis=0, tiled=False)
    outs, lses = [], []
    for h in range(heads):
        q_h = head(q_t, h)
        if h:
            q_h, outs[-1] = lax.optimization_barrier((q_h, outs[-1]))
        out_h, lse_h = attend(info, q_h, keys[h])
        outs.append(out_h)
        lses.append(lse_h)
    out_all = jnp.concatenate([o.astype(BF) for o in outs])
    mine_w, out_all = lax.optimization_barrier((mine_w, out_all))
    halves = [unpack_weights(w, half_hidden, here) for w in (mine_w, swap(mine_w, "c"))]
    expand_t, reduce_t, out_t = zip(*halves)
    att = lax.all_to_all(
        out_all, ALL, split_axis=1, concat_axis=0, axis_index_groups=groups, tiled=True
    )

    sides = (c, 1 - c)
    atts = [part(att, side, half_model, 0) for side in sides]
    wide = inputs.astype(F32)
    middle = wide + o_bias
    for a, w in zip(atts, out_t):
        middle = middle + mm("ft,mf->tm", a, w)
    unit2, root2 = normalise(middle)
    normed2 = (unit2 * gain2 + bias2).astype(BF)
    total = middle + r_bias
    grad_normed = 0.0
    acts, grads_a, grads_r, grads_e = [], [], [], []
    for side, w_e, w_r in zip(sides, expand_t, reduce_t):
        bias = part(e_bias, side, half_hidden, 1).reshape(-1)
        pre = mm("tm,hm->th", normed2, w_e) + bias
        act, pullback = jax.vjp(smooth_gelu, pre)
        act = act.astype(BF)
        total = total + mm("th,mh->tm", act, w_r)
        grads_r.append(mm("tm,th->mh", cotangent, act).astype(BF))
        grad_pre = pullback(mm("tm,mh->th", cotangent, w_r))[0].astype(BF)
        grads_a.append(mm("th,tm->hm", grad_pre, normed2).astype(BF))
        grads_e.append(jnp.sum(grad_pre.astype(F32), axis=0).reshape(shards, half_hidden))
        grad_normed = grad_normed + mm("th,hm->tm", grad_pre, w_e)
    result = total.astype(BF)
    cot = cotangent.astype(F32)
    grad_reduce_b = jnp.sum(cot, axis=0)
    grad_gain2 = jnp.sum(grad_normed * unit2, axis=0)
    grad_bias2 = jnp.sum(grad_normed, axis=0)
    grad_expand_b = in_order(c, grads_e[0], grads_e[1], 1)
    grad_middle = cot + normalise_back(grad_normed, unit2, root2, gain2)
    grad_branch = grad_middle.astype(BF)
    grad_out_b = jnp.sum(grad_branch.astype(F32), axis=0)
    grad_atts = [mm("mf,tm->ft", w, grad_branch).astype(BF) for w in out_t]
    grad_att = in_order(c, grad_atts[0], grad_atts[1], 0)
    grad_heads = lax.all_to_all(
        grad_att, ALL, split_axis=0, concat_axis=1, axis_index_groups=groups, tiled=True
    )
    grads_o = [mm("tm,ft->mf", grad_branch, a).astype(BF) for a in atts]

    packs = [
        pack_grads(e, w, o, shards) for e, w, o in zip(grads_a, grads_r, grads_o)
    ]
    sum_w = (packs[0].astype(F32) + swap(packs[1], "c").astype(F32)).astype(BF)
    sum_w = lax.psum_scatter(sum_w, WEIGHT_AXES, scatter_dimension=0, tiled=False)

    dqs, dkvs = [], []
    for h in range(heads):
        g_h = head(grad_heads, h)
        if h:
            g_h, dqs[-1] = lax.optimization_barrier((g_h, dqs[-1]))
        if h > 1:
            g_h, dkvs[h - 2] = lax.optimization_barrier((g_h, dkvs[h - 2]))
        dq_h, dkv_h = attend_back(info, head(q_t, h), g_h, outs[h], lses[h], keys[h])
        dqs.append(dq_h)
        if h == heads - 1:
            dkv_h, sum_w, dkvs[-1] = lax.optimization_barrier((dkv_h, sum_w, dkvs[-1]))
            dkvs.append(lax.psum_scatter(dkv_h, RING, scatter_dimension=0, tiled=True))
        else:
            pieces = lax.all_to_all(
                dkv_h.reshape(ring, depth * tokens, 128), RING, split_axis=0, concat_axis=0, tiled=True
            )
            dkvs.append(pieces)

    for h in range(heads - 1):
        dkvs[h] = jnp.sum(dkvs[h].astype(F32), axis=0).astype(BF)
    sum_w = swap_sum(sum_w, "y").astype(BF)
    grad_expand_w, grad_reduce_w, grad_out_w = unpack_grads(
        sum_w, swap(sum_w, "c"), c, half_hidden, here
    )

    dq = jnp.concatenate(dqs)
    dkv = jnp.concatenate(dkvs, axis=1)
    grad_w_q = mm("ft,tm->fm", dq, normed1)
    grad_w_kv = mm("tf,tm->fm", dkv, normed1).reshape(heads, 2, HEAD_DIM, model)
    grad_w = jnp.concatenate([grad_w_q, grad_w_kv.transpose(1, 0, 2, 3).reshape(2 * width, model)])
    grad_q_b = jnp.sum(dq.astype(F32), axis=1)
    grad_v_b = jnp.sum(dkv.astype(F32), axis=0).reshape(heads, 2, HEAD_DIM)[:, 1].reshape(width)
    part_norm = mm("ft,fm->tm", dq, w_q) + mm("tf,fm->tm", dkv, w_kv)
    grad_gain1 = jnp.sum(part_norm * unit1, axis=0)
    grad_bias1 = jnp.sum(part_norm, axis=0)
    grad_normed1 = lax.psum_scatter(
        part_norm.astype(BF), ALL, scatter_dimension=0, axis_index_groups=groups, tiled=True
    ).astype(F32)
    unit_in, root_in = normalise(wide)
    grad_in = (grad_middle + normalise_back(grad_normed1, unit_in, root_in, gain1)).astype(BF)

    placed_q = lax.dynamic_update_slice(jnp.zeros((model,), F32), grad_q_b, (z * width,))
    placed_v = lax.dynamic_update_slice(jnp.zeros((model,), F32), grad_v_b, (z * width,))
    small_grads = jnp.concatenate(
        [
            v.reshape(shards, -1)
            for v in (
                grad_gain1,
                grad_bias1,
                placed_q,
                placed_v,
                grad_out_b,
                grad_gain2,
                grad_bias2,
                grad_reduce_b,
                grad_expand_b,
            )
        ],
        axis=1,
    )
    grad_triple_w, flat = (send_triple if special else send_triple_whole)(grad_w, small_grads, at)
    vecs = [flat[i * here : (i + 1) * here] for i in range(8)]
    grad_e_b = flat[8 * here : 8 * here + hidden_here]
    return (
        result,
        grad_in,
        vecs[0],
        vecs[1],
        grad_triple_w,
        vecs[2],
        vecs[3],
        grad_out_w,
        vecs[4],
        vecs[5],
        vecs[6],
        grad_expand_w,
        grad_e_b,
        grad_reduce_w,
        vecs[7],
    )


def reduce_half(weight, c, half):
    pieces = weight.reshape(-1, 2, half, weight.shape[1])
    return part(pieces, c, 1, 1).reshape(-1, weight.shape[1]).T


def solution(mesh):
    fsdp, seq = mesh.shape["fsdp"], mesh.shape["seq"]
    wide = Mesh(
        mesh.devices.reshape(fsdp // GROUP, GROUP // 2, 2, seq // 2, 2), ("g", "z", "x", "y", "c")
    )
    rows = P(ALL, None)
    vector = P(WEIGHT_AXES)
    matrix = P(None, WEIGHT_AXES)
    return jax.shard_map(
        on_device,
        mesh=wide,
        in_specs=(
            rows,
            rows,
            vector,
            vector,
            matrix,
            vector,
            vector,
            matrix,
            vector,
            vector,
            vector,
            matrix,
            vector,
            matrix,
            vector,
        ),
        out_specs=(
            rows,
            rows,
            vector,
            vector,
            matrix,
            vector,
            vector,
            matrix,
            vector,
            vector,
            vector,
            matrix,
            vector,
            matrix,
            vector,
        ),
        check_vma=False,
    )
```

```python
import functools

import jax
import jax.numpy as jnp
from jax import lax
from jax.experimental import pallas as pl
from jax.experimental.pallas import tpu as pltpu
from jax.sharding import Mesh
from jax.sharding import PartitionSpec as P

HEADS = 12
HEAD_DIM = 64
GROUP = 8
EPSILON = 1e-05
NEG = -1e30
LOG2E = 1.4426950408889634
CH = 512
BF = jnp.bfloat16
F32 = jnp.float32
WEIGHT_AXES = ("g", "z", "x")
RING = ("x", "y", "c")
ALL = ("g", "z", "x", "y", "c")


def dotf(a, b):
    return lax.dot_general(a, b, (((1,), (0,)), ((), ())), preferred_element_type=F32)


def block_at(index):
    return pl.ds(pl.multiple_of(index * CH, CH), CH)


def fill_keys(kv_ref, wide, turned, first, ones):
    lane = lax.broadcasted_iota(jnp.int32, (CH, 128), 1)
    unit = jnp.where((lane >= 64) & (lane < 67), 1.0, 0.0).astype(BF)

    def body(i, _):
        at = block_at(i)
        block = kv_ref[at, :]
        wide[at, 0:128] = block
        wide[at, 128:256] = jnp.where(lane < 64, block, unit)
        turned[0:64, at] = block.T[first : first + 64]
        if ones:
            turned[64:80, at] = jnp.ones((16, CH), BF)
        return 0

    lax.fori_loop(0, kv_ref.shape[0] // CH, body, 0)


def split_low(value, count):
    parts = []
    for _ in range(count):
        part = value.astype(BF)
        parts.append(part)
        value = value - part.astype(F32)
    return parts


def pack_query(pack, query):
    hi, lo = split_low(query.astype(F32) * (LOG2E * 0.125), 2)
    pack[0:64, :] = hi
    pack[64:128, :] = jnp.zeros((64, CH), BF)
    pack[128:192, :] = lo
    pack[192:256, :] = jnp.zeros((64, CH), BF)


def pack_shift(pack, shift):
    parts = [jnp.broadcast_to(p.astype(F32), (16, CH)) for p in split_low(shift, 3)]
    at = lax.broadcasted_iota(jnp.int32, (16, CH), 0)
    rows = jnp.where(at == 0, parts[0], jnp.where(at == 1, parts[1], parts[2]))
    pack[192:208, :] = jnp.where(at < 3, rows, 0.0).astype(BF)


def flip_of(info, strip):
    return 7 * lax.rem(strip + info[1], 2)


def key_place(info, chunk, strips):
    strip = lax.div(chunk, 8)
    holder = lax.rem(chunk, 8) ^ flip_of(info, strip)
    return holder * strips + strip


def causal(scores):
    key = lax.broadcasted_iota(jnp.int32, scores.shape, 0)
    query = lax.broadcasted_iota(jnp.int32, scores.shape, 1)
    return jnp.where(key <= query, scores, NEG)


def forward_kernel(
    strips, unroll, r_ref, q_ref, kv_ref, out_ref, lse_ref, wide, turned, pack, top_s, acc
):
    i = pl.program_id(0)
    count = i * 8 + (r_ref[0] ^ flip_of(r_ref, i))

    @pl.when(i == 0)
    def _():
        fill_keys(kv_ref, wide, turned, 64, True)

    pack_query(pack, q_ref[...])
    top_s[...] = jnp.full(top_s.shape, NEG, F32)
    acc[...] = jnp.zeros(acc.shape, F32)

    def step(chunks, last):
        places = [block_at(key_place(r_ref, c, strips)) for c in chunks]
        scores = [dotf(wide[at, :], pack[...]) for at in places]
        if last:
            scores[-1] = causal(scores[-1])
        before = top_s[...]
        top = before
        for s in scores:
            top = jnp.maximum(top, jnp.max(s, axis=0, keepdims=True))
        total = acc[...] * jnp.exp2(before - top)
        for at, s in zip(places, scores):
            total = total + dotf(turned[:, at], jnp.exp2(s - top).astype(BF))
        acc[...] = total
        top_s[...] = top

    def many(t, _):
        step([t * unroll + u for u in range(unroll)], False)
        return 0

    def single(c, _):
        step([c], False)
        return 0

    rounds = lax.div(count, unroll)
    lax.fori_loop(0, rounds, many, 0)
    lax.fori_loop(rounds * unroll, count, single, 0)
    step([count], True)
    mass = acc[64:65, :]
    out_ref[...] = acc[0:64, :] / mass
    lse_ref[...] = jnp.broadcast_to(top_s[...] + jnp.log2(mass), lse_ref.shape)


def attend(r, query, kv, unroll=4):
    keys, rows = kv.shape[0], query.shape[1]
    strips = rows // CH
    return pl.pallas_call(
        functools.partial(forward_kernel, strips, unroll),
        grid=(strips,),
        in_specs=[
            pl.BlockSpec(memory_space=pltpu.SMEM),
            pl.BlockSpec((64, CH), lambda i: (0, i)),
            pl.BlockSpec((keys, 128), lambda i: (0, 0)),
        ],
        out_specs=[
            pl.BlockSpec((64, CH), lambda i: (0, i)),
            pl.BlockSpec((8, CH), lambda i: (0, i)),
        ],
        out_shape=[
            jax.ShapeDtypeStruct((64, rows), F32),
            jax.ShapeDtypeStruct((8, rows), F32),
        ],
        scratch_shapes=[
            pltpu.VMEM((keys, 256), BF),
            pltpu.VMEM((80, keys), BF),
            pltpu.VMEM((256, CH), BF),
            pltpu.VMEM((1, CH), F32),
            pltpu.VMEM((80, CH), F32),
        ],
        compiler_params=pltpu.CompilerParams(vmem_limit_bytes=56 * 2**20),
        cost_estimate=pl.CostEstimate(
            flops=15 * 10**9, bytes_accessed=8 * 2**20, transcendentals=0
        ),
    )(r, query, kv)


def backward_kernel(
    strips,
    unroll,
    r_ref,
    q_ref,
    g_ref,
    out_ref,
    lse_ref,
    kv_ref,
    dq_ref,
    dkv_ref,
    wide,
    turned,
    dkv,
    dq,
    q_pack,
    g_pack,
    q_rows,
    g_rows,
):
    i = pl.program_id(0)
    count = i * 8 + (r_ref[0] ^ flip_of(r_ref, i))

    @pl.when(i == 0)
    def _():
        fill_keys(kv_ref, wide, turned, 0, False)

        def clear(t, _):
            dkv[block_at(t), :] = jnp.zeros((CH, 128), F32)
            return 0

        lax.fori_loop(0, dkv.shape[0] // CH, clear, 0)

    query, grad = q_ref[...], g_ref[...]
    blank = jnp.zeros((64, CH), BF)
    pack_query(q_pack, query)
    pack_shift(q_pack, -lse_ref[0:1, :])
    g_pack[0:64, :] = blank
    g_pack[64:128, :] = grad
    g_pack[128:256, :] = jnp.zeros((128, CH), BF)
    pack_shift(g_pack, -jnp.sum(grad.astype(F32) * out_ref[...], axis=0, keepdims=True))
    q_rows[...] = jnp.concatenate([query * BF(0.125), blank]).T
    g_rows[...] = jnp.concatenate([blank, grad]).T
    dq[...] = jnp.zeros(dq.shape, F32)

    def step(chunks, last):
        places = [block_at(key_place(r_ref, c, strips)) for c in chunks]
        scores = [dotf(wide[at, :], q_pack[...]) for at in places]
        grads = [dotf(wide[at, :], g_pack[...]) for at in places]
        if last:
            scores[-1] = causal(scores[-1])
        total = dq[...]
        for at, s, g in zip(places, scores, grads):
            p = jnp.exp2(s)
            ds = (p * g).astype(BF)
            dkv[at, :] += dotf(p.astype(BF), g_rows[...]) + dotf(ds, q_rows[...])
            total = total + dotf(turned[:, at], ds)
        dq[...] = total

    def many(t, _):
        step([t * unroll + u for u in range(unroll)], False)
        return 0

    def single(c, _):
        step([c], False)
        return 0

    rounds = lax.div(count, unroll)
    lax.fori_loop(0, rounds, many, 0)
    if unroll > 1:
        lax.fori_loop(rounds * unroll, count, single, 0)
    step([count], True)
    dq_ref[...] = (dq[...] * 0.125).astype(dq_ref.dtype)

    @pl.when(i == strips - 1)
    def _():
        def write(t, _):
            dkv_ref[block_at(t), :] = dkv[block_at(t), :].astype(BF)
            return 0

        lax.fori_loop(0, dkv.shape[0] // CH, write, 0)


def attend_back(r, query, grad, out, lse, kv, unroll=2):
    keys, rows = kv.shape[0], query.shape[1]
    strips = rows // CH
    strip = pl.BlockSpec((64, CH), lambda i: (0, i))
    whole = pl.BlockSpec((keys, 128), lambda i: (0, 0))
    return pl.pallas_call(
        functools.partial(backward_kernel, strips, unroll),
        grid=(strips,),
        in_specs=[
            pl.BlockSpec(memory_space=pltpu.SMEM),
            strip,
            strip,
            strip,
            pl.BlockSpec((8, CH), lambda i: (0, i)),
            whole,
        ],
        out_specs=[strip, whole],
        out_shape=[
            jax.ShapeDtypeStruct((64, rows), BF),
            jax.ShapeDtypeStruct((keys, 128), BF),
        ],
        scratch_shapes=[
            pltpu.VMEM((keys, 256), BF),
            pltpu.VMEM((64, keys), BF),
            pltpu.VMEM((keys, 128), F32),
            pltpu.VMEM((64, CH), F32),
            pltpu.VMEM((256, CH), BF),
            pltpu.VMEM((256, CH), BF),
            pltpu.VMEM((CH, 128), BF),
            pltpu.VMEM((CH, 128), BF),
        ],
        compiler_params=pltpu.CompilerParams(vmem_limit_bytes=56 * 2**20),
        cost_estimate=pl.CostEstimate(
            flops=25 * 10**9, bytes_accessed=12 * 2**20, transcendentals=0
        ),
    )(r, query, grad, out, lse, kv)


def normalise(value):
    centre = value - jnp.mean(value, axis=-1, keepdims=True)
    spread = jnp.mean(centre * centre, axis=-1, keepdims=True)
    root = lax.rsqrt(spread + EPSILON)
    return centre * root, root


def normalise_back(grad, unit, root, gain):
    f = grad * gain
    first = jnp.mean(f, axis=-1, keepdims=True)
    second = jnp.mean(f * unit, axis=-1, keepdims=True)
    return root * (f - first - unit * second)


def smooth_gelu(value):
    return (
        0.5
        * value
        * (1.0 + jnp.tanh(0.7978845608028654 * (value + 0.044715 * value * value * value)))
    )


def mm(spec, a, b):
    return jnp.einsum(spec, a, b, preferred_element_type=F32)


def swap(array, axis):
    return lax.ppermute(array, axis, [(0, 1), (1, 0)])


def swap_sum(array, axis):
    return array.astype(F32) + swap(array, axis).astype(F32)


def in_order(at, own, other, axis):
    return jnp.where(
        at == 0, jnp.concatenate([own, other], axis), jnp.concatenate([other, own], axis)
    )


def part(array, index, size, axis):
    return lax.dynamic_slice_in_dim(array, index * size, size, axis)


def pad_rows(array, rows):
    return jnp.pad(array, ((0, rows - array.shape[0]), (0, 0)))


def spread_groups(blocks, depth, ring):
    return [
        [b * depth * ring + z * ring + (r if z % 2 == 0 else ring - 1 - r) for z in range(depth)]
        for b in range(blocks)
        for r in range(ring)
    ]


def pack_weights(expand, reduce, out, c):
    half_hidden = expand.shape[1] // 2
    model, here = out.shape
    e = part(expand.T, c, half_hidden, 0)
    w = reduce_half(reduce, c, half_hidden)
    o = part(out.T, c, model // 2, 1)
    return jnp.concatenate(
        [
            e,
            w[:, :model],
            w[:, model:],
            jnp.concatenate([o[: here // 2], o[here // 2 :]], axis=1),
        ]
    )


def unpack_weights(packed, half_hidden, here):
    shards, _, model = packed.shape
    first, second = half_hidden, half_hidden + here
    e = packed[:, :first].reshape(-1, model)
    w = jnp.concatenate(
        [
            packed[:, first:second].reshape(-1, model),
            packed[:, second : second + here].reshape(-1, model),
        ],
        axis=1,
    )
    o = packed[:, second + here :].reshape(shards, here // 2, 2, model // 2)
    return e, w, o.transpose(0, 2, 1, 3).reshape(-1, model // 2)


def pack_grads(e, w, o, shards):
    model = e.shape[1]
    here = model // shards
    o = o.reshape(shards, 2, here // 2, model // 2).transpose(0, 2, 1, 3)
    return jnp.concatenate(
        [
            e.reshape(shards, -1, model),
            w[:, :model].reshape(shards, here, model),
            w[:, model:].reshape(shards, here, model),
            o.reshape(shards, here // 2, model),
        ],
        axis=1,
    )


def unpack_grads(own, other, c, half_hidden, here):
    model = own.shape[1]
    first, second = half_hidden, half_hidden + here

    def reduce_of(rows):
        w = jnp.concatenate([rows[first:second], rows[second : second + here]], axis=1)
        return w.reshape(here, -1, 1, half_hidden)

    def out_of(rows):
        o = rows[second + here :]
        return jnp.concatenate([o[:, : model // 2], o[:, model // 2 :]])

    e = in_order(c, own[:first], other[:first], 0)
    w = in_order(c, reduce_of(own), reduce_of(other), 2).reshape(here, -1)
    o = in_order(c, out_of(own), out_of(other), 1)
    return e.T.astype(F32), w.T.astype(F32), o.T.astype(F32)


def fetch_triple(triple_weight, small, at):
    z, x, c = at
    turned = triple_weight.T
    three, model = turned.shape
    half = model // 2
    width = model // 4
    extra = small.shape[0] // half
    mine = jnp.concatenate([part(turned, c, half, 1), pad_rows(small.reshape(extra, half), 16)])
    both = in_order(x, mine[None], swap(mine, "x")[None], 0)
    pairs = both[:, :three].reshape(3, width, half)
    pairs = jnp.concatenate([pairs, jnp.zeros((1, width, half), BF)])
    slots = lax.dynamic_slice_in_dim(jnp.concatenate([pairs, pairs]), z, 4, 0)
    vectors = pad_rows(both[:, three : three + extra].reshape(2 * extra, half), 16)
    slots = jnp.concatenate([slots, jnp.broadcast_to(vectors, (4, 16, half))], axis=1)
    got = lax.all_to_all(slots, "z", split_axis=0, concat_axis=0, tiled=True)
    own = jnp.concatenate(
        [
            lax.dynamic_index_in_dim(got, (z + 4 * kind) // 3, 0, keepdims=False)[:width]
            for kind in range(3)
        ]
    )
    weights = in_order(c, own, swap(own, "c"), 1)
    return weights, got[:, width : width + 2 * extra].reshape(8, extra * half)


def fetch_triple_whole(triple_weight, small, at):
    z, x, c = at
    model = triple_weight.shape[0]
    width = model // 4
    whole = lax.all_gather(triple_weight.T, WEIGHT_AXES, axis=0, tiled=True)
    vectors = lax.all_gather(small, WEIGHT_AXES, axis=0, tiled=False)
    rows = [lax.dynamic_slice_in_dim(whole, k * model + z * width, width, 0) for k in range(3)]
    return jnp.concatenate(rows), vectors


def send_triple(grads, small, at):
    z, x, c = at
    model = grads.shape[1]
    half = model // 2
    width = model // 4
    three = 3 * width // 2
    extra = small.shape[1] // half
    low = grads.astype(BF)
    vectors = small.astype(BF).reshape(8 * extra, half)
    vectors = pad_rows(vectors, 32)
    mine = jnp.concatenate([part(low, c, half, 1), vectors])
    other = jnp.concatenate([part(low, 1 - c, half, 1), vectors])
    total = (mine.astype(F32) + swap(other, "c").astype(F32)).astype(BF)
    total = swap_sum(total, "y").astype(BF)
    by_depth = total[3 * width : 3 * width + 8 * extra].reshape(4, 2 * extra, half)
    by_depth = jnp.pad(by_depth, ((0, 0), (0, 16 - 2 * extra), (0, 0)))
    slots = jnp.zeros((4, width, half), BF)
    for kind in range(3):
        piece = total[kind * width : (kind + 1) * width][None]
        slots = lax.dynamic_update_slice(slots, piece, ((z + 4 * kind) // 3, 0, 0))
    got = lax.all_to_all(
        jnp.concatenate([slots, by_depth], axis=1), "z", split_axis=0, concat_axis=0, tiled=True
    )
    pairs = jnp.concatenate(
        [
            lax.dynamic_index_in_dim(got, (i - z) % 4, 0, keepdims=False)[:width]
            for i in range(3)
        ]
    )
    sums = jnp.sum(got[:, width : width + 2 * extra].astype(F32), axis=0).astype(BF)

    def portion(index):
        rows = part(pairs, index, three, 0)
        return jnp.concatenate([rows, pad_rows(part(sums, index, extra, 0), 16)])

    total = portion(x).astype(F32) + swap(portion(1 - x), "x").astype(F32)
    own = total[:three].astype(BF)
    shard = in_order(c, own, swap(own, "c"), 1).astype(F32)
    return shard.T, total[three : three + extra].reshape(-1)


def send_triple_whole(grads, small, at):
    z, x, c = at
    model = grads.shape[1]
    width = model // 4
    whole = jnp.zeros((3 * model, model), BF)
    for kind in range(3):
        piece = grads[kind * width : (kind + 1) * width].astype(BF)
        whole = lax.dynamic_update_slice(whole, piece, (kind * model + z * width, 0))
    shard = lax.psum_scatter(whole, WEIGHT_AXES, scatter_dimension=0, tiled=True)
    vectors = lax.psum_scatter(small, WEIGHT_AXES, scatter_dimension=0, tiled=False)
    shard = swap_sum(swap_sum(shard, "y").astype(BF), "c")
    return shard.T, swap_sum(swap_sum(vectors, "y"), "c")


def on_device(
    inputs,
    cotangent,
    first_gain,
    first_bias,
    triple_weight,
    query_bias,
    value_bias,
    out_weight,
    out_bias,
    second_gain,
    second_bias,
    expand_weight,
    expand_bias,
    reduce_weight,
    reduce_bias,
):
    tokens, model = inputs.shape
    hidden_here = expand_weight.shape[1]
    here = out_weight.shape[1]
    blocks, depth = lax.axis_size("g"), lax.axis_size("z")
    shards = blocks * depth * lax.axis_size("x")
    ring = lax.axis_size("x") * lax.axis_size("y") * lax.axis_size("c")
    z, x, y, c = [lax.axis_index(name).astype(jnp.int32) for name in ("z", "x", "y", "c")]
    at = (z, x, c)
    r = (x * lax.axis_size("y") + y) * lax.axis_size("c") + c
    heads = HEADS // depth
    width = heads * HEAD_DIM
    half_hidden = hidden_here // 2
    half_model = model // 2
    groups = spread_groups(blocks, depth, ring)
    info = jnp.stack([r, z % 2])
    special = shards == 8 and blocks == 1

    small = jnp.concatenate(
        [
            first_gain,
            first_bias,
            query_bias,
            value_bias,
            out_bias,
            second_gain,
            second_bias,
            reduce_bias,
            expand_bias,
        ]
    )
    x_all = lax.all_gather(inputs, ALL, axis_index_groups=groups, axis=0, tiled=True)
    weights, flat_small = (fetch_triple if special else fetch_triple_whole)(
        triple_weight, small, at
    )
    vectors = [flat_small[:, i * here : (i + 1) * here].reshape(model).astype(F32) for i in range(8)]
    gain1, bias1, q_bias, v_bias, o_bias, gain2, bias2, r_bias = vectors
    e_bias = flat_small[:, 8 * here : 8 * here + hidden_here].astype(F32)

    w_q = weights[:width]
    w_kv = weights[width:].reshape(2, heads, HEAD_DIM, model).transpose(1, 0, 2, 3)
    w_kv = w_kv.reshape(2 * width, model)
    b_q = part(q_bias, z, width, 0)
    b_v = part(v_bias, z, width, 0).reshape(heads, HEAD_DIM)
    b_kv = jnp.stack([jnp.zeros_like(b_v), b_v], axis=1).reshape(2 * width)

    unit1, _ = normalise(x_all.astype(F32))
    normed1 = (unit1 * gain1 + bias1).astype(BF)
    kv = (mm("tm,fm->tf", normed1, w_kv) + b_kv).astype(BF)
    q_t = (mm("fm,tm->ft", w_q, normed1) + b_q[:, None]).astype(BF)

    def head(array, h):
        return array[h * HEAD_DIM : (h + 1) * HEAD_DIM]

    def pair(h):
        return kv[:, h * 128 : (h + 1) * 128]

    keys = [lax.all_gather(pair(0), RING, axis=0, tiled=True)]
    for h in range(1, heads - 1):
        own_pair, keys[-1] = lax.optimization_barrier((pair(h), keys[-1]))
        keys.append(lax.all_gather(own_pair, RING, axis=0, tiled=True))
    copies = jnp.broadcast_to(pair(heads - 1), (ring,) + pair(0).shape)
    keys.append(
        lax.all_to_all(copies, RING, split_axis=0, concat_axis=0, tiled=True).reshape(-1, 128)
    )

    own_w = pack_weights(expand_weight, reduce_weight, out_weight, c)
    outs, lses = [], []
    for h in range(heads):
        q_h = head(q_t, h)
        if h:
            q_h, outs[-1] = lax.optimization_barrier((q_h, outs[-1]))
        out_h, lse_h = attend(info, q_h, keys[h])
        outs.append(out_h)
        lses.append(lse_h)
        if h == 0:
            own_w, keys[1], outs[0] = lax.optimization_barrier((own_w, keys[1], outs[0]))
            mine_w = lax.all_gather(own_w, WEIGHT_AXES, axis=0, tiled=False)

    def to_tokens(values):
        low = jnp.concatenate([v.astype(BF) for v in values])
        got = lax.all_to_all(
            low, ALL, split_axis=1, concat_axis=0, axis_index_groups=groups, tiled=True
        )
        return got.reshape(depth, low.shape[0], tokens)

    early = to_tokens(outs[:-1])
    late = outs[-1].astype(BF)
    mine_w, late, early = lax.optimization_barrier((mine_w, late, early))
    att = jnp.concatenate([early, to_tokens([late])], axis=1).reshape(model, tokens)
    w_all = jnp.concatenate([w_q, w_kv])
    w_all, mine_w = lax.optimization_barrier((w_all, mine_w))
    w_all = lax.all_gather(w_all, "z", axis=0, tiled=False)
    halves = [unpack_weights(w, half_hidden, here) for w in (mine_w, swap(mine_w, "c"))]
    expand_t, reduce_t, out_t = zip(*halves)

    sides = (c, 1 - c)
    atts = [part(att, side, half_model, 0) for side in sides]
    wide = inputs.astype(F32)
    middle = wide + o_bias
    for a, w in zip(atts, out_t):
        middle = middle + mm("ft,mf->tm", a, w)
    unit2, root2 = normalise(middle)
    normed2 = (unit2 * gain2 + bias2).astype(BF)
    total = middle + r_bias
    grad_normed = 0.0
    acts, grad_pres, grads_e = [], [], []
    for side, w_e, w_r in zip(sides, expand_t, reduce_t):
        bias = part(e_bias, side, half_hidden, 1).reshape(-1)
        pre = mm("tm,hm->th", normed2, w_e) + bias
        act, pullback = jax.vjp(smooth_gelu, pre)
        act = act.astype(BF)
        total = total + mm("th,mh->tm", act, w_r)
        acts.append(act)
        grad_pre = pullback(mm("tm,mh->th", cotangent, w_r))[0].astype(BF)
        grad_pres.append(grad_pre)
        grads_e.append(jnp.sum(grad_pre.astype(F32), axis=0).reshape(shards, half_hidden))
        grad_normed = grad_normed + mm("th,hm->tm", grad_pre, w_e)
    result = total.astype(BF)
    cot = cotangent.astype(F32)
    grad_reduce_b = jnp.sum(cot, axis=0)
    grad_gain2 = jnp.sum(grad_normed * unit2, axis=0)
    grad_bias2 = jnp.sum(grad_normed, axis=0)
    grad_expand_b = in_order(c, grads_e[0], grads_e[1], 1)
    grad_middle = cot + normalise_back(grad_normed, unit2, root2, gain2)
    grad_branch = grad_middle.astype(BF)
    grad_out_b = jnp.sum(grad_branch.astype(F32), axis=0)
    grad_atts = [mm("mf,tm->ft", w, grad_branch).astype(BF) for w in out_t]
    grad_att = in_order(c, grad_atts[0], grad_atts[1], 0)
    grad_att, acts, grad_pres = lax.optimization_barrier((grad_att, acts, grad_pres))
    by_head = grad_att.reshape(depth, heads, HEAD_DIM, tokens)

    def to_heads(first, last):
        got = lax.all_to_all(
            by_head[:, first:last].reshape(-1, tokens),
            ALL,
            split_axis=0,
            concat_axis=1,
            axis_index_groups=groups,
            tiled=True,
        )
        return got

    grad_first = to_heads(0, 1)
    grad_rest = to_heads(1, heads)
    grads_r = [mm("tm,th->mh", cotangent, act).astype(BF) for act in acts]
    grads_a = [mm("th,tm->hm", g, normed2).astype(BF) for g in grad_pres]
    grads_o = [mm("tm,ft->mf", grad_branch, a).astype(BF) for a in atts]

    packs = [
        pack_grads(e, w, o, shards) for e, w, o in zip(grads_a, grads_r, grads_o)
    ]
    sum_w = (packs[0].astype(F32) + swap(packs[1], "c").astype(F32)).astype(BF)
    sum_w = lax.psum_scatter(sum_w, WEIGHT_AXES, scatter_dimension=0, tiled=False)

    dqs, dkvs = [], []
    for h in range(heads):
        g_h = head(grad_rest, h - 1) if h else grad_first
        if h:
            g_h, dqs[-1] = lax.optimization_barrier((g_h, dqs[-1]))
        if h > 1:
            g_h, dkvs[h - 2] = lax.optimization_barrier((g_h, dkvs[h - 2]))
        dq_h, dkv_h = attend_back(info, head(q_t, h), g_h, outs[h], lses[h], keys[h])
        dqs.append(dq_h)
        if h == heads - 1:
            dkv_h, sum_w, dkvs[-1] = lax.optimization_barrier((dkv_h, sum_w, dkvs[-1]))
            dkvs.append(lax.psum_scatter(dkv_h, RING, scatter_dimension=0, tiled=True))
        else:
            pieces = lax.all_to_all(
                dkv_h.reshape(ring, depth * tokens, 128), RING, split_axis=0, concat_axis=0, tiled=True
            )
            dkvs.append(pieces)

    for h in range(heads - 1):
        dkvs[h] = jnp.sum(dkvs[h].astype(F32), axis=0).astype(BF)
    sum_w = swap_sum(sum_w, "y").astype(BF)
    grad_expand_w, grad_reduce_w, grad_out_w = unpack_grads(
        sum_w, swap(sum_w, "c"), c, half_hidden, here
    )

    unit_low = unit1.astype(BF)
    w_own = jnp.concatenate([w_q, w_kv])
    rest = (heads - 1) * 128 + width
    both = [
        jnp.concatenate([jnp.concatenate(dqs).T] + dkvs[:-1], axis=1),
        dkvs[-1],
    ]
    grad_w = jnp.concatenate([mm("tf,tm->fm", d, normed1) for d in both])
    grad_u = jnp.concatenate([mm("tf,tm->fm", d, unit_low) for d in both])
    grad_s = jnp.concatenate([jnp.sum(d.astype(F32), axis=0) for d in both])
    grad_gain1 = jnp.sum(w_own.astype(F32) * grad_u, axis=0)
    grad_bias1 = jnp.sum(w_own.astype(F32) * grad_s[:, None], axis=0)
    grad_q_b = grad_s[:width]
    grad_v_b = grad_s[width:].reshape(heads, 2, HEAD_DIM)[:, 1].reshape(width)
    grad_w_kv = grad_w[width:].reshape(heads, 2, HEAD_DIM, model)
    grad_w = jnp.concatenate(
        [grad_w[:width], grad_w_kv.transpose(1, 0, 2, 3).reshape(2 * width, model)]
    )
    grad_normed1 = 0.0
    for d, w in zip(both, (w_all[:, :rest], w_all[:, rest:])):
        got = lax.all_to_all(
            d, ALL, split_axis=0, concat_axis=0, axis_index_groups=groups, tiled=True
        ).reshape(depth, tokens, -1)
        for k in range(depth):
            grad_normed1 = grad_normed1 + mm("tf,fm->tm", got[k], w[k])
    unit_in, root_in = normalise(wide)
    grad_in = (grad_middle + normalise_back(grad_normed1, unit_in, root_in, gain1)).astype(BF)

    placed_q = lax.dynamic_update_slice(jnp.zeros((model,), F32), grad_q_b, (z * width,))
    placed_v = lax.dynamic_update_slice(jnp.zeros((model,), F32), grad_v_b, (z * width,))
    small_grads = jnp.concatenate(
        [
            v.reshape(shards, -1)
            for v in (
                grad_gain1,
                grad_bias1,
                placed_q,
                placed_v,
                grad_out_b,
                grad_gain2,
                grad_bias2,
                grad_reduce_b,
                grad_expand_b,
            )
        ],
        axis=1,
    )
    grad_triple_w, flat = (send_triple if special else send_triple_whole)(grad_w, small_grads, at)
    vecs = [flat[i * here : (i + 1) * here] for i in range(8)]
    grad_e_b = flat[8 * here : 8 * here + hidden_here]
    return (
        result,
        grad_in,
        vecs[0],
        vecs[1],
        grad_triple_w,
        vecs[2],
        vecs[3],
        grad_out_w,
        vecs[4],
        vecs[5],
        vecs[6],
        grad_expand_w,
        grad_e_b,
        grad_reduce_w,
        vecs[7],
    )


def reduce_half(weight, c, half):
    pieces = weight.reshape(-1, 2, half, weight.shape[1])
    return part(pieces, c, 1, 1).reshape(-1, weight.shape[1]).T


def solution(mesh):
    fsdp, seq = mesh.shape["fsdp"], mesh.shape["seq"]
    wide = Mesh(
        mesh.devices.reshape(fsdp // GROUP, GROUP // 2, 2, seq // 2, 2), ("g", "z", "x", "y", "c")
    )
    rows = P(ALL, None)
    vector = P(WEIGHT_AXES)
    matrix = P(None, WEIGHT_AXES)
    return jax.shard_map(
        on_device,
        mesh=wide,
        in_specs=(
            rows,
            rows,
            vector,
            vector,
            matrix,
            vector,
            vector,
            matrix,
            vector,
            vector,
            vector,
            matrix,
            vector,
            matrix,
            vector,
        ),
        out_specs=(
            rows,
            rows,
            vector,
            vector,
            matrix,
            vector,
            vector,
            matrix,
            vector,
            vector,
            vector,
            matrix,
            vector,
            matrix,
            vector,
        ),
        check_vma=False,
    )
```

```python
import functools

import jax
import jax.numpy as jnp
from jax import lax
from jax.experimental import pallas as pl
from jax.experimental.pallas import tpu as pltpu
from jax.sharding import Mesh
from jax.sharding import PartitionSpec as P

HEADS = 12
HEAD_DIM = 64
GROUP = 8
EPSILON = 1e-05
NEG = -1e30
LOG2E = 1.4426950408889634
CH = 512
BF = jnp.bfloat16
F32 = jnp.float32
WEIGHT_AXES = ("g", "z", "x")
RING = ("x", "y", "c")
ALL = ("g", "z", "x", "y", "c")


def dotf(a, b):
    return lax.dot_general(a, b, (((1,), (0,)), ((), ())), preferred_element_type=F32)


def block_at(index):
    return pl.ds(pl.multiple_of(index * CH, CH), CH)


def fill_keys(kv_ref, wide, turned, first, ones):
    lane = lax.broadcasted_iota(jnp.int32, (CH, 128), 1)
    unit = jnp.where((lane >= 64) & (lane < 67), 1.0, 0.0).astype(BF)

    def body(i, _):
        at = block_at(i)
        block = kv_ref[at, :]
        wide[at, 0:128] = block
        wide[at, 128:256] = jnp.where(lane < 64, block, unit)
        turned[0:64, at] = block.T[first : first + 64]
        if ones:
            turned[64:80, at] = jnp.ones((16, CH), BF)
        return 0

    lax.fori_loop(0, kv_ref.shape[0] // CH, body, 0)


def split_low(value, count):
    parts = []
    for _ in range(count):
        part = value.astype(BF)
        parts.append(part)
        value = value - part.astype(F32)
    return parts


def pack_query(pack, query):
    hi, lo = split_low(query.astype(F32) * (LOG2E * 0.125), 2)
    pack[0:64, :] = hi
    pack[64:128, :] = jnp.zeros((64, CH), BF)
    pack[128:192, :] = lo
    pack[192:256, :] = jnp.zeros((64, CH), BF)


def pack_shift(pack, shift):
    parts = [jnp.broadcast_to(p.astype(F32), (16, CH)) for p in split_low(shift, 3)]
    at = lax.broadcasted_iota(jnp.int32, (16, CH), 0)
    rows = jnp.where(at == 0, parts[0], jnp.where(at == 1, parts[1], parts[2]))
    pack[192:208, :] = jnp.where(at < 3, rows, 0.0).astype(BF)


def flip_of(info, strip):
    return 7 * lax.rem(strip + info[1], 2)


def key_place(info, chunk, strips):
    strip = lax.div(chunk, 8)
    holder = lax.rem(chunk, 8) ^ flip_of(info, strip)
    return holder * strips + strip


def causal(scores):
    key = lax.broadcasted_iota(jnp.int32, scores.shape, 0)
    query = lax.broadcasted_iota(jnp.int32, scores.shape, 1)
    return jnp.where(key <= query, scores, NEG)


def forward_kernel(
    strips, unroll, r_ref, q_ref, kv_ref, out_ref, lse_ref, wide, turned, pack, top_s, acc
):
    i = pl.program_id(0)
    count = i * 8 + (r_ref[0] ^ flip_of(r_ref, i))

    @pl.when(i == 0)
    def _():
        fill_keys(kv_ref, wide, turned, 64, True)

    pack_query(pack, q_ref[...])
    top_s[...] = jnp.full(top_s.shape, NEG, F32)
    acc[...] = jnp.zeros(acc.shape, F32)

    def step(chunks, last):
        places = [block_at(key_place(r_ref, c, strips)) for c in chunks]
        scores = [dotf(wide[at, :], pack[...]) for at in places]
        if last:
            scores[-1] = causal(scores[-1])
        before = top_s[...]
        top = before
        for s in scores:
            top = jnp.maximum(top, jnp.max(s, axis=0, keepdims=True))
        total = acc[...] * jnp.exp2(before - top)
        for at, s in zip(places, scores):
            total = total + dotf(turned[:, at], jnp.exp2(s - top).astype(BF))
        acc[...] = total
        top_s[...] = top

    def many(t, _):
        step([t * unroll + u for u in range(unroll)], False)
        return 0

    def single(c, _):
        step([c], False)
        return 0

    rounds = lax.div(count, unroll)
    lax.fori_loop(0, rounds, many, 0)
    lax.fori_loop(rounds * unroll, count, single, 0)
    step([count], True)
    mass = acc[64:65, :]
    out_ref[...] = acc[0:64, :] / mass
    lse_ref[...] = jnp.broadcast_to(top_s[...] + jnp.log2(mass), lse_ref.shape)


def attend(r, query, kv, column, unroll=4):
    keys, rows = kv.shape[0], query.shape[1]
    strips = rows // CH
    return pl.pallas_call(
        functools.partial(forward_kernel, strips, unroll),
        grid=(strips,),
        in_specs=[
            pl.BlockSpec(memory_space=pltpu.SMEM),
            pl.BlockSpec((64, CH), lambda i: (0, i)),
            pl.BlockSpec((keys, 128), lambda i: (0, column)),
        ],
        out_specs=[
            pl.BlockSpec((64, CH), lambda i: (0, i)),
            pl.BlockSpec((8, CH), lambda i: (0, i)),
        ],
        out_shape=[
            jax.ShapeDtypeStruct((64, rows), F32),
            jax.ShapeDtypeStruct((8, rows), F32),
        ],
        scratch_shapes=[
            pltpu.VMEM((keys, 256), BF),
            pltpu.VMEM((80, keys), BF),
            pltpu.VMEM((256, CH), BF),
            pltpu.VMEM((1, CH), F32),
            pltpu.VMEM((80, CH), F32),
        ],
        compiler_params=pltpu.CompilerParams(vmem_limit_bytes=56 * 2**20),
        cost_estimate=pl.CostEstimate(
            flops=15 * 10**9, bytes_accessed=8 * 2**20, transcendentals=0
        ),
    )(r, query, kv)


def backward_kernel(
    strips,
    unroll,
    r_ref,
    q_ref,
    g_ref,
    out_ref,
    lse_ref,
    kv_ref,
    dq_ref,
    dkv_ref,
    wide,
    turned,
    dkv,
    dq,
    q_pack,
    g_pack,
    q_rows,
    g_rows,
):
    i = pl.program_id(0)
    count = i * 8 + (r_ref[0] ^ flip_of(r_ref, i))

    @pl.when(i == 0)
    def _():
        fill_keys(kv_ref, wide, turned, 0, False)

        def clear(t, _):
            dkv[block_at(t), :] = jnp.zeros((CH, 128), F32)
            return 0

        lax.fori_loop(0, dkv.shape[0] // CH, clear, 0)

    query, grad = q_ref[...], g_ref[...]
    blank = jnp.zeros((64, CH), BF)
    pack_query(q_pack, query)
    pack_shift(q_pack, -lse_ref[0:1, :])
    g_pack[0:64, :] = blank
    g_pack[64:128, :] = grad
    g_pack[128:256, :] = jnp.zeros((128, CH), BF)
    pack_shift(g_pack, -jnp.sum(grad.astype(F32) * out_ref[...], axis=0, keepdims=True))
    q_rows[...] = jnp.concatenate([query * BF(0.125), blank]).T
    g_rows[...] = jnp.concatenate([blank, grad]).T
    dq[...] = jnp.zeros(dq.shape, F32)

    def step(chunks, last):
        places = [block_at(key_place(r_ref, c, strips)) for c in chunks]
        scores = [dotf(wide[at, :], q_pack[...]) for at in places]
        grads = [dotf(wide[at, :], g_pack[...]) for at in places]
        if last:
            scores[-1] = causal(scores[-1])
        total = dq[...]
        for at, s, g in zip(places, scores, grads):
            p = jnp.exp2(s)
            ds = (p * g).astype(BF)
            dkv[at, :] += dotf(p.astype(BF), g_rows[...]) + dotf(ds, q_rows[...])
            total = total + dotf(turned[:, at], ds)
        dq[...] = total

    def many(t, _):
        step([t * unroll + u for u in range(unroll)], False)
        return 0

    def single(c, _):
        step([c], False)
        return 0

    rounds = lax.div(count, unroll)
    lax.fori_loop(0, rounds, many, 0)
    if unroll > 1:
        lax.fori_loop(rounds * unroll, count, single, 0)
    step([count], True)
    dq_ref[...] = (dq[...] * 0.125).astype(dq_ref.dtype)

    @pl.when(i == strips - 1)
    def _():
        def write(t, _):
            dkv_ref[block_at(t), :] = dkv[block_at(t), :].astype(BF)
            return 0

        lax.fori_loop(0, dkv.shape[0] // CH, write, 0)


def attend_back(r, query, grad, out, lse, kv, column, unroll=2):
    keys, rows = kv.shape[0], query.shape[1]
    strips = rows // CH
    strip = pl.BlockSpec((64, CH), lambda i: (0, i))
    whole = pl.BlockSpec((keys, 128), lambda i: (0, 0))
    return pl.pallas_call(
        functools.partial(backward_kernel, strips, unroll),
        grid=(strips,),
        in_specs=[
            pl.BlockSpec(memory_space=pltpu.SMEM),
            strip,
            strip,
            strip,
            pl.BlockSpec((8, CH), lambda i: (0, i)),
            pl.BlockSpec((keys, 128), lambda i: (0, column)),
        ],
        out_specs=[strip, whole],
        out_shape=[
            jax.ShapeDtypeStruct((64, rows), BF),
            jax.ShapeDtypeStruct((keys, 128), BF),
        ],
        scratch_shapes=[
            pltpu.VMEM((keys, 256), BF),
            pltpu.VMEM((64, keys), BF),
            pltpu.VMEM((keys, 128), F32),
            pltpu.VMEM((64, CH), F32),
            pltpu.VMEM((256, CH), BF),
            pltpu.VMEM((256, CH), BF),
            pltpu.VMEM((CH, 128), BF),
            pltpu.VMEM((CH, 128), BF),
        ],
        compiler_params=pltpu.CompilerParams(vmem_limit_bytes=56 * 2**20),
        cost_estimate=pl.CostEstimate(
            flops=25 * 10**9, bytes_accessed=12 * 2**20, transcendentals=0
        ),
    )(r, query, grad, out, lse, kv)


def normalise(value):
    centre = value - jnp.mean(value, axis=-1, keepdims=True)
    spread = jnp.mean(centre * centre, axis=-1, keepdims=True)
    root = lax.rsqrt(spread + EPSILON)
    return centre * root, root


def normalise_back(grad, unit, root, gain):
    f = grad * gain
    first = jnp.mean(f, axis=-1, keepdims=True)
    second = jnp.mean(f * unit, axis=-1, keepdims=True)
    return root * (f - first - unit * second)


def smooth_gelu(value):
    return (
        0.5
        * value
        * (1.0 + jnp.tanh(0.7978845608028654 * (value + 0.044715 * value * value * value)))
    )


def mm(spec, a, b):
    return jnp.einsum(spec, a, b, preferred_element_type=F32)


def swap(array, axis):
    return lax.ppermute(array, axis, [(0, 1), (1, 0)])


def swap_sum(array, axis):
    return array.astype(F32) + swap(array, axis).astype(F32)


def in_order(at, own, other, axis):
    return jnp.where(
        at == 0, jnp.concatenate([own, other], axis), jnp.concatenate([other, own], axis)
    )


def part(array, index, size, axis):
    return lax.dynamic_slice_in_dim(array, index * size, size, axis)


def pad_rows(array, rows):
    return jnp.pad(array, ((0, rows - array.shape[0]), (0, 0)))


def spread_groups(blocks, depth, ring):
    return [
        [b * depth * ring + z * ring + (r if z % 2 == 0 else ring - 1 - r) for z in range(depth)]
        for b in range(blocks)
        for r in range(ring)
    ]


def pack_weights(expand, reduce, out, c):
    half_hidden = expand.shape[1] // 2
    model, here = out.shape
    e = part(expand.T, c, half_hidden, 0)
    w = reduce_half(reduce, c, half_hidden)
    o = part(out.T, c, model // 2, 1)
    return jnp.concatenate(
        [
            e,
            w[:, :model],
            w[:, model:],
            jnp.concatenate([o[: here // 2], o[here // 2 :]], axis=1),
        ]
    )


def unpack_weights(packed, half_hidden, here):
    shards, _, model = packed.shape
    first, second = half_hidden, half_hidden + here
    e = packed[:, :first].reshape(-1, model)
    w = jnp.concatenate(
        [
            packed[:, first:second].reshape(-1, model),
            packed[:, second : second + here].reshape(-1, model),
        ],
        axis=1,
    )
    o = packed[:, second + here :].reshape(shards, here // 2, 2, model // 2)
    return e, w, o.transpose(0, 2, 1, 3).reshape(-1, model // 2)


def pack_grads(e, w, o, shards):
    model = e.shape[1]
    here = model // shards
    o = o.reshape(shards, 2, here // 2, model // 2).transpose(0, 2, 1, 3)
    return jnp.concatenate(
        [
            e.reshape(shards, -1, model),
            w[:, :model].reshape(shards, here, model),
            w[:, model:].reshape(shards, here, model),
            o.reshape(shards, here // 2, model),
        ],
        axis=1,
    )


def unpack_grads(own, other, c, half_hidden, here):
    model = own.shape[1]
    first, second = half_hidden, half_hidden + here

    def reduce_of(rows):
        w = jnp.concatenate([rows[first:second], rows[second : second + here]], axis=1)
        return w.reshape(here, -1, 1, half_hidden)

    def out_of(rows):
        o = rows[second + here :]
        return jnp.concatenate([o[:, : model // 2], o[:, model // 2 :]])

    e = in_order(c, own[:first], other[:first], 0)
    w = in_order(c, reduce_of(own), reduce_of(other), 2).reshape(here, -1)
    o = in_order(c, out_of(own), out_of(other), 1)
    return e.T.astype(F32), w.T.astype(F32), o.T.astype(F32)


def sum_pieces(parts):
    return jnp.sum(parts.astype(F32), axis=0).astype(BF)


def exchange(values, z, groups):
    depth = len(groups[0])
    blocks = values.reshape(depth, -1, values.shape[1])
    got = [lax.dynamic_index_in_dim(blocks, z, 0, keepdims=False)]
    for k in range(1, depth):
        sent = lax.dynamic_index_in_dim(blocks, (z + k) % depth, 0, keepdims=False)
        pairs = [(g[i], g[(i + k) % depth]) for g in groups for i in range(depth)]
        got.append(lax.ppermute(sent, ALL, pairs))
    return got


def fetch_triple(triple_weight, small, at):
    z, x, c = at
    turned = triple_weight.T
    three, model = turned.shape
    half = model // 2
    width = model // 4
    extra = small.shape[0] // half
    mine = jnp.concatenate([part(turned, c, half, 1), pad_rows(small.reshape(extra, half), 16)])
    both = in_order(x, mine[None], swap(mine, "x")[None], 0)
    pairs = both[:, :three].reshape(3, width, half)
    pairs = jnp.concatenate([pairs, jnp.zeros((1, width, half), BF)])
    slots = lax.dynamic_slice_in_dim(jnp.concatenate([pairs, pairs]), z, 4, 0)
    vectors = pad_rows(both[:, three : three + extra].reshape(2 * extra, half), 16)
    slots = jnp.concatenate([slots, jnp.broadcast_to(vectors, (4, 16, half))], axis=1)
    got = lax.all_to_all(slots, "z", split_axis=0, concat_axis=0, tiled=True)
    own = jnp.concatenate(
        [
            lax.dynamic_index_in_dim(got, (z + 4 * kind) // 3, 0, keepdims=False)[:width]
            for kind in range(3)
        ]
    )
    weights = in_order(c, own, swap(own, "c"), 1)
    return weights, got[:, width : width + 2 * extra].reshape(8, extra * half)


def fetch_triple_whole(triple_weight, small, at):
    z, x, c = at
    model = triple_weight.shape[0]
    width = model // 4
    whole = lax.all_gather(triple_weight.T, WEIGHT_AXES, axis=0, tiled=True)
    vectors = lax.all_gather(small, WEIGHT_AXES, axis=0, tiled=False)
    rows = [lax.dynamic_slice_in_dim(whole, k * model + z * width, width, 0) for k in range(3)]
    return jnp.concatenate(rows), vectors


def send_triple(grads, small, at):
    z, x, c = at
    model = grads.shape[1]
    half = model // 2
    width = model // 4
    three = 3 * width // 2
    extra = small.shape[1] // half
    low = grads.astype(BF)
    vectors = small.astype(BF).reshape(8 * extra, half)
    vectors = pad_rows(vectors, 32)
    mine = jnp.concatenate([part(low, c, half, 1), vectors])
    other = jnp.concatenate([part(low, 1 - c, half, 1), vectors])
    total = (mine.astype(F32) + swap(other, "c").astype(F32)).astype(BF)
    total = swap_sum(total, "y").astype(BF)
    by_depth = total[3 * width : 3 * width + 8 * extra].reshape(4, 2 * extra, half)
    by_depth = jnp.pad(by_depth, ((0, 0), (0, 16 - 2 * extra), (0, 0)))
    slots = jnp.zeros((4, width, half), BF)
    for kind in range(3):
        piece = total[kind * width : (kind + 1) * width][None]
        slots = lax.dynamic_update_slice(slots, piece, ((z + 4 * kind) // 3, 0, 0))
    got = lax.all_to_all(
        jnp.concatenate([slots, by_depth], axis=1), "z", split_axis=0, concat_axis=0, tiled=True
    )
    pairs = jnp.concatenate(
        [
            lax.dynamic_index_in_dim(got, (i - z) % 4, 0, keepdims=False)[:width]
            for i in range(3)
        ]
    )
    sums = jnp.sum(got[:, width : width + 2 * extra].astype(F32), axis=0).astype(BF)

    def portion(index):
        rows = part(pairs, index, three, 0)
        return jnp.concatenate([rows, pad_rows(part(sums, index, extra, 0), 16)])

    total = portion(x).astype(F32) + swap(portion(1 - x), "x").astype(F32)
    own = total[:three].astype(BF)
    shard = in_order(c, own, swap(own, "c"), 1).astype(F32)
    return shard.T, total[three : three + extra].reshape(-1)


def send_triple_whole(grads, small, at):
    z, x, c = at
    model = grads.shape[1]
    width = model // 4
    whole = jnp.zeros((3 * model, model), BF)
    for kind in range(3):
        piece = grads[kind * width : (kind + 1) * width].astype(BF)
        whole = lax.dynamic_update_slice(whole, piece, (kind * model + z * width, 0))
    shard = lax.psum_scatter(whole, WEIGHT_AXES, scatter_dimension=0, tiled=True)
    vectors = lax.psum_scatter(small, WEIGHT_AXES, scatter_dimension=0, tiled=False)
    shard = swap_sum(swap_sum(shard, "y").astype(BF), "c")
    return shard.T, swap_sum(swap_sum(vectors, "y"), "c")


def on_device(
    inputs,
    cotangent,
    first_gain,
    first_bias,
    triple_weight,
    query_bias,
    value_bias,
    out_weight,
    out_bias,
    second_gain,
    second_bias,
    expand_weight,
    expand_bias,
    reduce_weight,
    reduce_bias,
):
    tokens, model = inputs.shape
    hidden_here = expand_weight.shape[1]
    here = out_weight.shape[1]
    blocks, depth = lax.axis_size("g"), lax.axis_size("z")
    shards = blocks * depth * lax.axis_size("x")
    ring = lax.axis_size("x") * lax.axis_size("y") * lax.axis_size("c")
    z, x, y, c = [lax.axis_index(name).astype(jnp.int32) for name in ("z", "x", "y", "c")]
    at = (z, x, c)
    r = (x * lax.axis_size("y") + y) * lax.axis_size("c") + c
    heads = HEADS // depth
    width = heads * HEAD_DIM
    half_hidden = hidden_here // 2
    half_model = model // 2
    groups = spread_groups(blocks, depth, ring)
    info = jnp.stack([r, z % 2])
    special = shards == 8 and blocks == 1

    small = jnp.concatenate(
        [
            first_gain,
            first_bias,
            query_bias,
            value_bias,
            out_bias,
            second_gain,
            second_bias,
            reduce_bias,
            expand_bias,
        ]
    )
    x_all = lax.all_gather(inputs, ALL, axis_index_groups=groups, axis=0, tiled=True)
    weights, flat_small = (fetch_triple if special else fetch_triple_whole)(
        triple_weight, small, at
    )
    vectors = [flat_small[:, i * here : (i + 1) * here].reshape(model).astype(F32) for i in range(8)]
    gain1, bias1, q_bias, v_bias, o_bias, gain2, bias2, r_bias = vectors
    e_bias = flat_small[:, 8 * here : 8 * here + hidden_here].astype(F32)

    w_q = weights[:width]
    w_kv = weights[width:].reshape(2, heads, HEAD_DIM, model).transpose(1, 0, 2, 3)
    w_kv = w_kv.reshape(2 * width, model)
    b_q = part(q_bias, z, width, 0)
    b_v = part(v_bias, z, width, 0).reshape(heads, HEAD_DIM)
    b_kv = jnp.stack([jnp.zeros_like(b_v), b_v], axis=1).reshape(2 * width)

    unit1, _ = normalise(x_all.astype(F32))
    normed1 = (unit1 * gain1 + bias1).astype(BF)
    kv = (mm("tm,fm->tf", normed1, w_kv) + b_kv).astype(BF)
    q_t = (mm("fm,tm->ft", w_q, normed1) + b_q[:, None]).astype(BF)

    def head(array, h):
        return array[h * HEAD_DIM : (h + 1) * HEAD_DIM]

    def pair(h):
        return kv[:, h * 128 : (h + 1) * 128]

    keys = [lax.all_gather(pair(0), RING, axis=0, tiled=True)]
    rest_pairs, keys[0] = lax.optimization_barrier((kv[:, 128:], keys[0]))
    keys.append(lax.all_gather(rest_pairs, RING, axis=0, tiled=True))

    own_w = pack_weights(expand_weight, reduce_weight, out_weight, c)
    outs, lses = [], []
    for h in range(heads):
        q_h = head(q_t, h)
        if h:
            q_h, outs[-1] = lax.optimization_barrier((q_h, outs[-1]))
        out_h, lse_h = attend(info, q_h, keys[min(h, 1)], max(h - 1, 0))
        outs.append(out_h)
        lses.append(lse_h)
        if h == 0:
            own_w, keys[1], outs[0] = lax.optimization_barrier((own_w, keys[1], outs[0]))
            mine_w = lax.all_gather(own_w, WEIGHT_AXES, axis=0, tiled=False)

    def to_tokens(values):
        low = jnp.concatenate([v.astype(BF) for v in values])
        got = lax.all_to_all(
            low, ALL, split_axis=1, concat_axis=0, axis_index_groups=groups, tiled=True
        )
        return got.reshape(depth, low.shape[0], tokens)

    early = to_tokens(outs[:-1])
    late = outs[-1].astype(BF)
    mine_w, late, early = lax.optimization_barrier((mine_w, late, early))
    att = jnp.concatenate([early, to_tokens([late])], axis=1).reshape(model, tokens)
    w_own = jnp.concatenate(
        [w_q[:128], w_kv[:128], w_q[128:], w_kv[128:256], w_kv[256:]]
    )
    w_all, mine_w = lax.optimization_barrier((w_own, mine_w))
    w_all = lax.all_gather(w_all, "z", axis=0, tiled=False)
    halves = [unpack_weights(w, half_hidden, here) for w in (mine_w, swap(mine_w, "c"))]
    expand_t, reduce_t, out_t = zip(*halves)

    sides = (c, 1 - c)
    atts = [part(att, side, half_model, 0) for side in sides]
    wide = inputs.astype(F32)
    middle = wide + o_bias
    for a, w in zip(atts, out_t):
        middle = middle + mm("ft,mf->tm", a, w)
    unit2, root2 = normalise(middle)
    normed2 = (unit2 * gain2 + bias2).astype(BF)
    total = middle + r_bias
    grad_normed = 0.0
    acts, grad_pres, grads_e = [], [], []
    for side, w_e, w_r in zip(sides, expand_t, reduce_t):
        bias = part(e_bias, side, half_hidden, 1).reshape(-1)
        pre = mm("tm,hm->th", normed2, w_e) + bias
        act, pullback = jax.vjp(smooth_gelu, pre)
        act = act.astype(BF)
        total = total + mm("th,mh->tm", act, w_r)
        acts.append(act)
        grad_pre = pullback(mm("tm,mh->th", cotangent, w_r))[0].astype(BF)
        grad_pres.append(grad_pre)
        grads_e.append(jnp.sum(grad_pre.astype(F32), axis=0).reshape(shards, half_hidden))
        grad_normed = grad_normed + mm("th,hm->tm", grad_pre, w_e)
    result = total.astype(BF)
    cot = cotangent.astype(F32)
    grad_reduce_b = jnp.sum(cot, axis=0)
    grad_gain2 = jnp.sum(grad_normed * unit2, axis=0)
    grad_bias2 = jnp.sum(grad_normed, axis=0)
    grad_expand_b = in_order(c, grads_e[0], grads_e[1], 1)
    grad_middle = cot + normalise_back(grad_normed, unit2, root2, gain2)
    grad_branch = grad_middle.astype(BF)
    grad_out_b = jnp.sum(grad_branch.astype(F32), axis=0)
    grad_atts = [mm("mf,tm->ft", w, grad_branch).astype(BF) for w in out_t]
    grad_att = in_order(c, grad_atts[0], grad_atts[1], 0)
    grad_att, acts, grad_pres = lax.optimization_barrier((grad_att, acts, grad_pres))
    by_head = grad_att.reshape(depth, heads, HEAD_DIM, tokens)

    def to_heads(first, last):
        got = lax.all_to_all(
            by_head[:, first:last].reshape(-1, tokens),
            ALL,
            split_axis=0,
            concat_axis=1,
            axis_index_groups=groups,
            tiled=True,
        )
        return got

    grad_first = to_heads(0, 1)
    grad_rest = to_heads(1, heads)
    grads_r = [mm("tm,th->mh", cotangent, act).astype(BF) for act in acts]
    grads_a = [mm("th,tm->hm", g, normed2).astype(BF) for g in grad_pres]
    grads_o = [mm("tm,ft->mf", grad_branch, a).astype(BF) for a in atts]

    packs = [
        pack_grads(e, w, o, shards) for e, w, o in zip(grads_a, grads_r, grads_o)
    ]
    sum_w = (packs[0].astype(F32) + swap(packs[1], "c").astype(F32)).astype(BF)
    sum_w = lax.psum_scatter(sum_w, WEIGHT_AXES, scatter_dimension=0, tiled=False)

    dqs, dkvs = [], []
    for h in range(heads):
        g_h = head(grad_rest, h - 1) if h else grad_first
        if h:
            g_h, dqs[-1] = lax.optimization_barrier((g_h, dqs[-1]))
        if h == heads - 1:
            first = sum_pieces(dkvs[0])
            pieces = [jnp.concatenate([jnp.concatenate(dqs).T, first], axis=1)]
            g_h, sum_w, first_piece = lax.optimization_barrier((g_h, sum_w, pieces[0]))
            pieces[0] = first_piece
            got = [exchange(first_piece, z, groups)]
            swapped = swap(sum_w, "y")
        dq_h, dkv_h = attend_back(
            info, head(q_t, h), g_h, outs[h], lses[h], keys[min(h, 1)], max(h - 1, 0)
        )
        dqs.append(dq_h)
        if h == heads - 1:
            dkv_h, swapped, dkvs[-1], got[0] = lax.optimization_barrier(
                (dkv_h, swapped, dkvs[-1], got[0])
            )
            dkvs.append(lax.psum_scatter(dkv_h, RING, scatter_dimension=0, tiled=True))
        else:
            parts = lax.all_to_all(
                dkv_h.reshape(ring, depth * tokens, 128), RING, split_axis=0, concat_axis=0, tiled=True
            )
            dkvs.append(parts)

    sum_w = (sum_w.astype(F32) + swapped.astype(F32)).astype(BF)
    grad_expand_w, grad_reduce_w, grad_out_w = unpack_grads(
        sum_w, swap(sum_w, "c"), c, half_hidden, here
    )

    unit_low = unit1.astype(BF)
    pieces.append(jnp.concatenate([dqs[-1].T, sum_pieces(dkvs[1])], axis=1))
    pieces.append(dkvs[2])
    got += [exchange(d, z, groups) for d in pieces[1:]]
    grad_w = jnp.concatenate([mm("tf,tm->fm", d, normed1) for d in pieces])
    grad_u = jnp.concatenate([mm("tf,tm->fm", d, unit_low) for d in pieces])
    grad_s = jnp.concatenate([jnp.sum(d.astype(F32), axis=0) for d in pieces])
    grad_gain1 = jnp.sum(w_own.astype(F32) * grad_u, axis=0)
    grad_bias1 = jnp.sum(w_own.astype(F32) * grad_s[:, None], axis=0)

    def of_kind(values, kind):
        starts = ((0, 64, 256), (128, 320, 448), (192, 384, 512))[kind]
        return jnp.concatenate([values[at : at + HEAD_DIM] for at in starts])

    grad_q_b = of_kind(grad_s, 0)
    grad_v_b = of_kind(grad_s, 2)
    grad_w = jnp.concatenate([of_kind(grad_w, kind) for kind in range(3)])
    grad_normed1 = 0.0
    at_row = 0
    for blocks_got in got:
        size = blocks_got[0].shape[1]
        for k, block in enumerate(blocks_got):
            w = lax.dynamic_index_in_dim(w_all, (z - k) % depth, 0, keepdims=False)
            grad_normed1 = grad_normed1 + mm("tf,fm->tm", block, w[at_row : at_row + size])
        at_row += size
    unit_in, root_in = normalise(wide)
    grad_in = (grad_middle + normalise_back(grad_normed1, unit_in, root_in, gain1)).astype(BF)

    placed_q = lax.dynamic_update_slice(jnp.zeros((model,), F32), grad_q_b, (z * width,))
    placed_v = lax.dynamic_update_slice(jnp.zeros((model,), F32), grad_v_b, (z * width,))
    small_grads = jnp.concatenate(
        [
            v.reshape(shards, -1)
            for v in (
                grad_gain1,
                grad_bias1,
                placed_q,
                placed_v,
                grad_out_b,
                grad_gain2,
                grad_bias2,
                grad_reduce_b,
                grad_expand_b,
            )
        ],
        axis=1,
    )
    grad_triple_w, flat = (send_triple if special else send_triple_whole)(grad_w, small_grads, at)
    vecs = [flat[i * here : (i + 1) * here] for i in range(8)]
    grad_e_b = flat[8 * here : 8 * here + hidden_here]
    return (
        result,
        grad_in,
        vecs[0],
        vecs[1],
        grad_triple_w,
        vecs[2],
        vecs[3],
        grad_out_w,
        vecs[4],
        vecs[5],
        vecs[6],
        grad_expand_w,
        grad_e_b,
        grad_reduce_w,
        vecs[7],
    )


def reduce_half(weight, c, half):
    pieces = weight.reshape(-1, 2, half, weight.shape[1])
    return part(pieces, c, 1, 1).reshape(-1, weight.shape[1]).T


def solution(mesh):
    fsdp, seq = mesh.shape["fsdp"], mesh.shape["seq"]
    wide = Mesh(
        mesh.devices.reshape(fsdp // GROUP, GROUP // 2, 2, seq // 2, 2), ("g", "z", "x", "y", "c")
    )
    rows = P(ALL, None)
    vector = P(WEIGHT_AXES)
    matrix = P(None, WEIGHT_AXES)
    return jax.shard_map(
        on_device,
        mesh=wide,
        in_specs=(
            rows,
            rows,
            vector,
            vector,
            matrix,
            vector,
            vector,
            matrix,
            vector,
            vector,
            vector,
            matrix,
            vector,
            matrix,
            vector,
        ),
        out_specs=(
            rows,
            rows,
            vector,
            vector,
            matrix,
            vector,
            vector,
            matrix,
            vector,
            vector,
            vector,
            matrix,
            vector,
            matrix,
            vector,
        ),
        check_vma=False,
    )
```

```python
import functools

import jax
import jax.numpy as jnp
from jax import lax
from jax.experimental import pallas as pl
from jax.experimental.pallas import tpu as pltpu
from jax.sharding import Mesh
from jax.sharding import PartitionSpec as P

HEADS = 12
HEAD_DIM = 64
GROUP = 8
EPSILON = 1e-05
NEG = -1e30
LOG2E = 1.4426950408889634
CH = 512
BF = jnp.bfloat16
F32 = jnp.float32
WEIGHT_AXES = ("g", "z", "x")
RING = ("x", "y", "c")
ALL = ("g", "z", "x", "y", "c")


def dotf(a, b):
    return lax.dot_general(a, b, (((1,), (0,)), ((), ())), preferred_element_type=F32)


def block_at(index):
    return pl.ds(pl.multiple_of(index * CH, CH), CH)


def fill_keys(kv_ref, wide, turned, first, ones):
    lane = lax.broadcasted_iota(jnp.int32, (CH, 128), 1)
    unit = jnp.where((lane >= 64) & (lane < 67), 1.0, 0.0).astype(BF)

    def body(i, _):
        at = block_at(i)
        block = kv_ref[at, :]
        wide[at, 0:128] = block
        wide[at, 128:256] = jnp.where(lane < 64, block, unit)
        turned[0:64, at] = block.T[first : first + 64]
        if ones:
            turned[64:80, at] = jnp.ones((16, CH), BF)
        return 0

    lax.fori_loop(0, kv_ref.shape[0] // CH, body, 0)


def split_low(value, count):
    parts = []
    for _ in range(count):
        part = value.astype(BF)
        parts.append(part)
        value = value - part.astype(F32)
    return parts


def pack_query(pack, query):
    hi, lo = split_low(query.astype(F32) * (LOG2E * 0.125), 2)
    pack[0:64, :] = hi
    pack[64:128, :] = jnp.zeros((64, CH), BF)
    pack[128:192, :] = lo
    pack[192:256, :] = jnp.zeros((64, CH), BF)


def pack_shift(pack, shift):
    parts = [jnp.broadcast_to(p.astype(F32), (16, CH)) for p in split_low(shift, 3)]
    at = lax.broadcasted_iota(jnp.int32, (16, CH), 0)
    rows = jnp.where(at == 0, parts[0], jnp.where(at == 1, parts[1], parts[2]))
    pack[192:208, :] = jnp.where(at < 3, rows, 0.0).astype(BF)


def flip_of(info, strip):
    return 7 * lax.rem(strip + info[1], 2)


def key_place(info, chunk, strips):
    strip = lax.div(chunk, 8)
    holder = lax.rem(chunk, 8) ^ flip_of(info, strip)
    return holder * strips + strip


def causal(scores):
    key = lax.broadcasted_iota(jnp.int32, scores.shape, 0)
    query = lax.broadcasted_iota(jnp.int32, scores.shape, 1)
    return jnp.where(key <= query, scores, NEG)


def forward_kernel(
    strips, unroll, r_ref, q_ref, kv_ref, out_ref, lse_ref, wide, turned, pack, top_s, acc
):
    i = pl.program_id(0)
    count = i * 8 + (r_ref[0] ^ flip_of(r_ref, i))

    @pl.when(i == 0)
    def _():
        fill_keys(kv_ref, wide, turned, 64, True)

    pack_query(pack, q_ref[...])
    top_s[...] = jnp.full(top_s.shape, NEG, F32)
    acc[...] = jnp.zeros(acc.shape, F32)

    def step(chunks, last):
        places = [block_at(key_place(r_ref, c, strips)) for c in chunks]
        scores = [dotf(wide[at, :], pack[...]) for at in places]
        if last:
            scores[-1] = causal(scores[-1])
        before = top_s[...]
        top = before
        for s in scores:
            top = jnp.maximum(top, jnp.max(s, axis=0, keepdims=True))
        total = acc[...] * jnp.exp2(before - top)
        for at, s in zip(places, scores):
            total = total + dotf(turned[:, at], jnp.exp2(s - top).astype(BF))
        acc[...] = total
        top_s[...] = top

    def many(t, _):
        step([t * unroll + u for u in range(unroll)], False)
        return 0

    def single(c, _):
        step([c], False)
        return 0

    rounds = lax.div(count, unroll)
    lax.fori_loop(0, rounds, many, 0)
    lax.fori_loop(rounds * unroll, count, single, 0)
    step([count], True)
    mass = acc[64:65, :]
    out_ref[...] = acc[0:64, :] / mass
    lse_ref[...] = jnp.broadcast_to(top_s[...] + jnp.log2(mass), lse_ref.shape)


def attend(r, query, kv, column, unroll=4):
    keys, rows = kv.shape[0], query.shape[1]
    strips = rows // CH
    return pl.pallas_call(
        functools.partial(forward_kernel, strips, unroll),
        grid=(strips,),
        in_specs=[
            pl.BlockSpec(memory_space=pltpu.SMEM),
            pl.BlockSpec((64, CH), lambda i: (0, i)),
            pl.BlockSpec((keys, 128), lambda i: (0, column)),
        ],
        out_specs=[
            pl.BlockSpec((64, CH), lambda i: (0, i)),
            pl.BlockSpec((8, CH), lambda i: (0, i)),
        ],
        out_shape=[
            jax.ShapeDtypeStruct((64, rows), F32),
            jax.ShapeDtypeStruct((8, rows), F32),
        ],
        scratch_shapes=[
            pltpu.VMEM((keys, 256), BF),
            pltpu.VMEM((80, keys), BF),
            pltpu.VMEM((256, CH), BF),
            pltpu.VMEM((1, CH), F32),
            pltpu.VMEM((80, CH), F32),
        ],
        compiler_params=pltpu.CompilerParams(vmem_limit_bytes=56 * 2**20),
        cost_estimate=pl.CostEstimate(
            flops=15 * 10**9, bytes_accessed=8 * 2**20, transcendentals=0
        ),
    )(r, query, kv)


def backward_kernel(
    strips,
    unroll,
    r_ref,
    q_ref,
    g_ref,
    out_ref,
    lse_ref,
    kv_ref,
    dq_ref,
    dkv_ref,
    wide,
    turned,
    dkv,
    dq,
    q_pack,
    g_pack,
    q_rows,
    g_rows,
):
    i = pl.program_id(0)
    count = i * 8 + (r_ref[0] ^ flip_of(r_ref, i))

    @pl.when(i == 0)
    def _():
        fill_keys(kv_ref, wide, turned, 0, False)

        def clear(t, _):
            dkv[block_at(t), :] = jnp.zeros((CH, 128), F32)
            return 0

        lax.fori_loop(0, dkv.shape[0] // CH, clear, 0)

    query, grad = q_ref[...], g_ref[...]
    blank = jnp.zeros((64, CH), BF)
    pack_query(q_pack, query)
    pack_shift(q_pack, -lse_ref[0:1, :])
    g_pack[0:64, :] = blank
    g_pack[64:128, :] = grad
    g_pack[128:256, :] = jnp.zeros((128, CH), BF)
    pack_shift(g_pack, -jnp.sum(grad.astype(F32) * out_ref[...], axis=0, keepdims=True))
    q_rows[...] = jnp.concatenate([query * BF(0.125), blank]).T
    g_rows[...] = jnp.concatenate([blank, grad]).T
    dq[...] = jnp.zeros(dq.shape, F32)

    def step(chunks, last):
        places = [block_at(key_place(r_ref, c, strips)) for c in chunks]
        scores = [dotf(wide[at, :], q_pack[...]) for at in places]
        grads = [dotf(wide[at, :], g_pack[...]) for at in places]
        if last:
            scores[-1] = causal(scores[-1])
        total = dq[...]
        for at, s, g in zip(places, scores, grads):
            p = jnp.exp2(s)
            ds = (p * g).astype(BF)
            dkv[at, :] += dotf(p.astype(BF), g_rows[...]) + dotf(ds, q_rows[...])
            total = total + dotf(turned[:, at], ds)
        dq[...] = total

    def many(t, _):
        step([t * unroll + u for u in range(unroll)], False)
        return 0

    def single(c, _):
        step([c], False)
        return 0

    rounds = lax.div(count, unroll)
    lax.fori_loop(0, rounds, many, 0)
    if unroll > 1:
        lax.fori_loop(rounds * unroll, count, single, 0)
    step([count], True)
    dq_ref[...] = (dq[...] * 0.125).astype(dq_ref.dtype)

    @pl.when(i == strips - 1)
    def _():
        def write(t, _):
            dkv_ref[block_at(t), :] = dkv[block_at(t), :].astype(BF)
            return 0

        lax.fori_loop(0, dkv.shape[0] // CH, write, 0)


def attend_back(r, query, grad, out, lse, kv, column, unroll=2):
    keys, rows = kv.shape[0], query.shape[1]
    strips = rows // CH
    strip = pl.BlockSpec((64, CH), lambda i: (0, i))
    whole = pl.BlockSpec((keys, 128), lambda i: (0, 0))
    return pl.pallas_call(
        functools.partial(backward_kernel, strips, unroll),
        grid=(strips,),
        in_specs=[
            pl.BlockSpec(memory_space=pltpu.SMEM),
            strip,
            strip,
            strip,
            pl.BlockSpec((8, CH), lambda i: (0, i)),
            pl.BlockSpec((keys, 128), lambda i: (0, column)),
        ],
        out_specs=[strip, whole],
        out_shape=[
            jax.ShapeDtypeStruct((64, rows), BF),
            jax.ShapeDtypeStruct((keys, 128), BF),
        ],
        scratch_shapes=[
            pltpu.VMEM((keys, 256), BF),
            pltpu.VMEM((64, keys), BF),
            pltpu.VMEM((keys, 128), F32),
            pltpu.VMEM((64, CH), F32),
            pltpu.VMEM((256, CH), BF),
            pltpu.VMEM((256, CH), BF),
            pltpu.VMEM((CH, 128), BF),
            pltpu.VMEM((CH, 128), BF),
        ],
        compiler_params=pltpu.CompilerParams(vmem_limit_bytes=56 * 2**20),
        cost_estimate=pl.CostEstimate(
            flops=25 * 10**9, bytes_accessed=12 * 2**20, transcendentals=0
        ),
    )(r, query, grad, out, lse, kv)


def normalise(value):
    centre = value - jnp.mean(value, axis=-1, keepdims=True)
    spread = jnp.mean(centre * centre, axis=-1, keepdims=True)
    root = lax.rsqrt(spread + EPSILON)
    return centre * root, root


def normalise_back(grad, unit, root, gain):
    f = grad * gain
    first = jnp.mean(f, axis=-1, keepdims=True)
    second = jnp.mean(f * unit, axis=-1, keepdims=True)
    return root * (f - first - unit * second)


def smooth_gelu(value):
    return (
        0.5
        * value
        * (1.0 + jnp.tanh(0.7978845608028654 * (value + 0.044715 * value * value * value)))
    )


def mm(spec, a, b):
    return jnp.einsum(spec, a, b, preferred_element_type=F32)


def swap(array, axis):
    return lax.ppermute(array, axis, [(0, 1), (1, 0)])


def swap_sum(array, axis):
    return array.astype(F32) + swap(array, axis).astype(F32)


def in_order(at, own, other, axis):
    return jnp.where(
        at == 0, jnp.concatenate([own, other], axis), jnp.concatenate([other, own], axis)
    )


def part(array, index, size, axis):
    return lax.dynamic_slice_in_dim(array, index * size, size, axis)


def pad_rows(array, rows):
    return jnp.pad(array, ((0, rows - array.shape[0]), (0, 0)))


def spread_groups(blocks, depth, ring):
    return [
        [b * depth * ring + z * ring + (r if z % 2 == 0 else ring - 1 - r) for z in range(depth)]
        for b in range(blocks)
        for r in range(ring)
    ]


def pack_weights(expand, reduce, out, c):
    half_hidden = expand.shape[1] // 2
    model, here = out.shape
    e = part(expand.T, c, half_hidden, 0)
    w = reduce_half(reduce, c, half_hidden)
    o = part(out.T, c, model // 2, 1)
    return jnp.concatenate(
        [
            e,
            w[:, :model],
            w[:, model:],
            jnp.concatenate([o[: here // 2], o[here // 2 :]], axis=1),
        ]
    )


def unpack_weights(packed, half_hidden, here):
    shards, _, model = packed.shape
    first, second = half_hidden, half_hidden + here
    e = packed[:, :first].reshape(-1, model)
    w = jnp.concatenate(
        [
            packed[:, first:second].reshape(-1, model),
            packed[:, second : second + here].reshape(-1, model),
        ],
        axis=1,
    )
    o = packed[:, second + here :].reshape(shards, here // 2, 2, model // 2)
    return e, w, o.transpose(0, 2, 1, 3).reshape(-1, model // 2)


def pack_grads(e, w, o, shards):
    model = e.shape[1]
    here = model // shards
    o = o.reshape(shards, 2, here // 2, model // 2).transpose(0, 2, 1, 3)
    return jnp.concatenate(
        [
            e.reshape(shards, -1, model),
            w[:, :model].reshape(shards, here, model),
            w[:, model:].reshape(shards, here, model),
            o.reshape(shards, here // 2, model),
        ],
        axis=1,
    )


def unpack_grads(own, other, c, half_hidden, here):
    model = own.shape[1]
    first, second = half_hidden, half_hidden + here

    def reduce_of(rows):
        w = jnp.concatenate([rows[first:second], rows[second : second + here]], axis=1)
        return w.reshape(here, -1, 1, half_hidden)

    def out_of(rows):
        o = rows[second + here :]
        return jnp.concatenate([o[:, : model // 2], o[:, model // 2 :]])

    e = in_order(c, own[:first], other[:first], 0)
    w = in_order(c, reduce_of(own), reduce_of(other), 2).reshape(here, -1)
    o = in_order(c, out_of(own), out_of(other), 1)
    return e.T.astype(F32), w.T.astype(F32), o.T.astype(F32)


def sum_pieces(parts):
    return jnp.sum(parts.astype(F32), axis=0).astype(BF)


def exchange(values, z, groups):
    depth = len(groups[0])
    blocks = values.reshape(depth, -1, values.shape[1])
    got = [lax.dynamic_index_in_dim(blocks, z, 0, keepdims=False)]
    for k in range(1, depth):
        sent = lax.dynamic_index_in_dim(blocks, (z + k) % depth, 0, keepdims=False)
        pairs = [(g[i], g[(i + k) % depth]) for g in groups for i in range(depth)]
        got.append(lax.ppermute(sent, ALL, pairs))
    return got


def fetch_triple(triple_weight, small, at):
    z, x, c = at
    turned = triple_weight.T
    three, model = turned.shape
    half = model // 2
    width = model // 4
    extra = small.shape[0] // half
    mine = jnp.concatenate([part(turned, c, half, 1), pad_rows(small.reshape(extra, half), 16)])
    both = in_order(x, mine[None], swap(mine, "x")[None], 0)
    pairs = both[:, :three].reshape(3, width, half)
    pairs = jnp.concatenate([pairs, jnp.zeros((1, width, half), BF)])
    slots = lax.dynamic_slice_in_dim(jnp.concatenate([pairs, pairs]), z, 4, 0)
    vectors = pad_rows(both[:, three : three + extra].reshape(2 * extra, half), 16)
    slots = jnp.concatenate([slots, jnp.broadcast_to(vectors, (4, 16, half))], axis=1)
    got = lax.all_to_all(slots, "z", split_axis=0, concat_axis=0, tiled=True)
    own = jnp.concatenate(
        [
            lax.dynamic_index_in_dim(got, (z + 4 * kind) // 3, 0, keepdims=False)[:width]
            for kind in range(3)
        ]
    )
    weights = in_order(c, own, swap(own, "c"), 1)
    return weights, got[:, width : width + 2 * extra].reshape(8, extra * half)


def fetch_triple_whole(triple_weight, small, at):
    z, x, c = at
    model = triple_weight.shape[0]
    width = model // 4
    whole = lax.all_gather(triple_weight.T, WEIGHT_AXES, axis=0, tiled=True)
    vectors = lax.all_gather(small, WEIGHT_AXES, axis=0, tiled=False)
    rows = [lax.dynamic_slice_in_dim(whole, k * model + z * width, width, 0) for k in range(3)]
    return jnp.concatenate(rows), vectors


def send_rows(grads, small, at):
    z, x, c = at
    model = grads.shape[1]
    half = model // 2
    width = grads.shape[0] // 3
    low = grads.astype(BF)
    mine, other = part(low, c, half, 1), part(low, 1 - c, half, 1)
    extra = 0
    if small is not None:
        extra = small.shape[1] // half
        vectors = pad_rows(small.astype(BF).reshape(8 * extra, half), 32)
        mine = jnp.concatenate([mine, vectors])
        other = jnp.concatenate([other, vectors])
    total = (mine.astype(F32) + swap(other, "c").astype(F32)).astype(BF)
    total = swap_sum(total, "y").astype(BF)
    slots = jnp.zeros((4, width, half), BF)
    for kind in range(3):
        piece = total[kind * width : (kind + 1) * width][None]
        slots = lax.dynamic_update_slice(slots, piece, ((z + 4 * kind) // 3, 0, 0))
    if extra:
        by_depth = total[3 * width : 3 * width + 8 * extra].reshape(4, 2 * extra, half)
        by_depth = jnp.pad(by_depth, ((0, 0), (0, 16 - 2 * extra), (0, 0)))
        slots = jnp.concatenate([slots, by_depth], axis=1)
    got = lax.all_to_all(slots, "z", split_axis=0, concat_axis=0, tiled=True)
    rows = jnp.concatenate(
        [
            lax.dynamic_index_in_dim(got, (i - z) % 4, 0, keepdims=False)[:width]
            for i in range(3)
        ]
    )
    if extra:
        sums = jnp.sum(got[:, width : width + 2 * extra].astype(F32), axis=0).astype(BF)
        rows = jnp.concatenate([rows, pad_rows(sums, 16)])
    total = swap_sum(rows, "x")
    pairs = total[: 3 * width].astype(BF).reshape(3, width, half)
    if extra:
        return pairs, part(total[3 * width : 3 * width + 2 * extra], x, extra, 0).reshape(-1)
    return pairs


def send_triple(grads, small, at, early):
    z, x, c = at
    late, vectors = send_rows(grads, small, at)
    pairs = jnp.concatenate([early, late], axis=1)
    own = part(pairs.reshape(-1, pairs.shape[2]), x, 3 * pairs.shape[1] // 2, 0)
    shard = in_order(c, own, swap(own, "c"), 1).astype(F32)
    return shard.T, vectors


def send_triple_whole(grads, small, at):
    z, x, c = at
    model = grads.shape[1]
    width = model // 4
    whole = jnp.zeros((3 * model, model), BF)
    for kind in range(3):
        piece = grads[kind * width : (kind + 1) * width].astype(BF)
        whole = lax.dynamic_update_slice(whole, piece, (kind * model + z * width, 0))
    shard = lax.psum_scatter(whole, WEIGHT_AXES, scatter_dimension=0, tiled=True)
    vectors = lax.psum_scatter(small, WEIGHT_AXES, scatter_dimension=0, tiled=False)
    shard = swap_sum(swap_sum(shard, "y").astype(BF), "c")
    return shard.T, swap_sum(swap_sum(vectors, "y"), "c")


def on_device(
    inputs,
    cotangent,
    first_gain,
    first_bias,
    triple_weight,
    query_bias,
    value_bias,
    out_weight,
    out_bias,
    second_gain,
    second_bias,
    expand_weight,
    expand_bias,
    reduce_weight,
    reduce_bias,
):
    tokens, model = inputs.shape
    hidden_here = expand_weight.shape[1]
    here = out_weight.shape[1]
    blocks, depth = lax.axis_size("g"), lax.axis_size("z")
    shards = blocks * depth * lax.axis_size("x")
    ring = lax.axis_size("x") * lax.axis_size("y") * lax.axis_size("c")
    z, x, y, c = [lax.axis_index(name).astype(jnp.int32) for name in ("z", "x", "y", "c")]
    at = (z, x, c)
    r = (x * lax.axis_size("y") + y) * lax.axis_size("c") + c
    heads = HEADS // depth
    width = heads * HEAD_DIM
    half_hidden = hidden_here // 2
    half_model = model // 2
    groups = spread_groups(blocks, depth, ring)
    info = jnp.stack([r, z % 2])
    special = shards == 8 and blocks == 1

    small = jnp.concatenate(
        [
            first_gain,
            first_bias,
            query_bias,
            value_bias,
            out_bias,
            second_gain,
            second_bias,
            reduce_bias,
            expand_bias,
        ]
    )
    x_all = lax.all_gather(inputs, ALL, axis_index_groups=groups, axis=0, tiled=True)
    weights, flat_small = (fetch_triple if special else fetch_triple_whole)(
        triple_weight, small, at
    )
    vectors = [flat_small[:, i * here : (i + 1) * here].reshape(model).astype(F32) for i in range(8)]
    gain1, bias1, q_bias, v_bias, o_bias, gain2, bias2, r_bias = vectors
    e_bias = flat_small[:, 8 * here : 8 * here + hidden_here].astype(F32)

    w_q = weights[:width]
    w_kv = weights[width:].reshape(2, heads, HEAD_DIM, model).transpose(1, 0, 2, 3)
    w_kv = w_kv.reshape(2 * width, model)
    b_q = part(q_bias, z, width, 0)
    b_v = part(v_bias, z, width, 0).reshape(heads, HEAD_DIM)
    b_kv = jnp.stack([jnp.zeros_like(b_v), b_v], axis=1).reshape(2 * width)

    unit1, _ = normalise(x_all.astype(F32))
    normed1 = (unit1 * gain1 + bias1).astype(BF)
    kv = (mm("tm,fm->tf", normed1, w_kv) + b_kv).astype(BF)
    q_t = (mm("fm,tm->ft", w_q, normed1) + b_q[:, None]).astype(BF)

    def head(array, h):
        return array[h * HEAD_DIM : (h + 1) * HEAD_DIM]

    def pair(h):
        return kv[:, h * 128 : (h + 1) * 128]

    keys = [lax.all_gather(pair(0), RING, axis=0, tiled=True)]
    rest_pairs, keys[0] = lax.optimization_barrier((kv[:, 128:], keys[0]))
    keys.append(lax.all_gather(rest_pairs, RING, axis=0, tiled=True))

    own_w = pack_weights(expand_weight, reduce_weight, out_weight, c)
    outs, lses = [], []
    for h in range(heads):
        q_h = head(q_t, h)
        if h:
            q_h, outs[-1] = lax.optimization_barrier((q_h, outs[-1]))
        out_h, lse_h = attend(info, q_h, keys[min(h, 1)], max(h - 1, 0))
        outs.append(out_h)
        lses.append(lse_h)
        if h == 0:
            own_w, keys[1], outs[0] = lax.optimization_barrier((own_w, keys[1], outs[0]))
            mine_w = lax.all_gather(own_w, WEIGHT_AXES, axis=0, tiled=False)

    def to_tokens(values):
        low = jnp.concatenate([v.astype(BF) for v in values])
        got = lax.all_to_all(
            low, ALL, split_axis=1, concat_axis=0, axis_index_groups=groups, tiled=True
        )
        return got.reshape(depth, low.shape[0], tokens)

    early = to_tokens(outs[:-1])
    late = outs[-1].astype(BF)
    mine_w, late, early = lax.optimization_barrier((mine_w, late, early))
    att = jnp.concatenate([early, to_tokens([late])], axis=1).reshape(model, tokens)
    w_own = jnp.concatenate(
        [w_q[:128], w_kv[:128], w_q[128:], w_kv[128:256], w_kv[256:]]
    )
    w_all, mine_w = lax.optimization_barrier((w_own, mine_w))
    w_all = lax.all_gather(w_all, "z", axis=0, tiled=False)
    halves = [unpack_weights(w, half_hidden, here) for w in (mine_w, swap(mine_w, "c"))]
    expand_t, reduce_t, out_t = zip(*halves)

    sides = (c, 1 - c)
    atts = [part(att, side, half_model, 0) for side in sides]
    wide = inputs.astype(F32)
    middle = wide + o_bias
    for a, w in zip(atts, out_t):
        middle = middle + mm("ft,mf->tm", a, w)
    unit2, root2 = normalise(middle)
    normed2 = (unit2 * gain2 + bias2).astype(BF)
    total = middle + r_bias
    grad_normed = 0.0
    acts, grad_pres, grads_e = [], [], []
    for side, w_e, w_r in zip(sides, expand_t, reduce_t):
        bias = part(e_bias, side, half_hidden, 1).reshape(-1)
        pre = mm("tm,hm->th", normed2, w_e) + bias
        act, pullback = jax.vjp(smooth_gelu, pre)
        act = act.astype(BF)
        total = total + mm("th,mh->tm", act, w_r)
        acts.append(act)
        grad_pre = pullback(mm("tm,mh->th", cotangent, w_r))[0].astype(BF)
        grad_pres.append(grad_pre)
        grads_e.append(jnp.sum(grad_pre.astype(F32), axis=0).reshape(shards, half_hidden))
        grad_normed = grad_normed + mm("th,hm->tm", grad_pre, w_e)
    result = total.astype(BF)
    cot = cotangent.astype(F32)
    grad_reduce_b = jnp.sum(cot, axis=0)
    grad_gain2 = jnp.sum(grad_normed * unit2, axis=0)
    grad_bias2 = jnp.sum(grad_normed, axis=0)
    grad_expand_b = in_order(c, grads_e[0], grads_e[1], 1)
    grad_middle = cot + normalise_back(grad_normed, unit2, root2, gain2)
    grad_branch = grad_middle.astype(BF)
    grad_out_b = jnp.sum(grad_branch.astype(F32), axis=0)
    grad_atts = [mm("mf,tm->ft", w, grad_branch).astype(BF) for w in out_t]
    grad_att = in_order(c, grad_atts[0], grad_atts[1], 0)
    grad_att, acts, grad_pres = lax.optimization_barrier((grad_att, acts, grad_pres))
    grad_heads = lax.all_to_all(
        grad_att, ALL, split_axis=0, concat_axis=1, axis_index_groups=groups, tiled=True
    )
    grads_r = [mm("tm,th->mh", cotangent, act).astype(BF) for act in acts]
    grads_a = [mm("th,tm->hm", g, normed2).astype(BF) for g in grad_pres]
    grads_o = [mm("tm,ft->mf", grad_branch, a).astype(BF) for a in atts]

    packs = [
        pack_grads(e, w, o, shards) for e, w, o in zip(grads_a, grads_r, grads_o)
    ]
    swapped_w = swap(packs[1], "c")
    swapped_w, grad_heads = lax.optimization_barrier((swapped_w, grad_heads))
    sum_w = (packs[0].astype(F32) + swapped_w.astype(F32)).astype(BF)
    sum_w = lax.psum_scatter(sum_w, WEIGHT_AXES, scatter_dimension=0, tiled=False)

    dqs, dkvs = [], []
    for h in range(heads):
        g_h = head(grad_heads, h)
        if h:
            g_h, dqs[-1] = lax.optimization_barrier((g_h, dqs[-1]))
        if h == heads - 1:
            first = sum_pieces(dkvs[0])
            pieces = [jnp.concatenate([jnp.concatenate(dqs).T, first], axis=1)]
            g_h, sum_w, first_piece = lax.optimization_barrier((g_h, sum_w, pieces[0]))
            pieces[0] = first_piece
            got = [exchange(first_piece, z, groups)]
            swapped = swap(sum_w, "y")
        dq_h, dkv_h = attend_back(
            info, head(q_t, h), g_h, outs[h], lses[h], keys[min(h, 1)], max(h - 1, 0)
        )
        dqs.append(dq_h)
        if h == heads - 1:
            dkv_h, swapped, dkvs[-1], got[0] = lax.optimization_barrier(
                (dkv_h, swapped, dkvs[-1], got[0])
            )
            dkvs.append(lax.psum_scatter(dkv_h, RING, scatter_dimension=0, tiled=True))
        else:
            parts = lax.all_to_all(
                dkv_h.reshape(ring, depth * tokens, 128), RING, split_axis=0, concat_axis=0, tiled=True
            )
            dkvs.append(parts)

    sum_w = (sum_w.astype(F32) + swapped.astype(F32)).astype(BF)
    grad_expand_w, grad_reduce_w, grad_out_w = unpack_grads(
        sum_w, swap(sum_w, "c"), c, half_hidden, here
    )

    unit_low = unit1.astype(BF)
    pieces.append(jnp.concatenate([dqs[-1].T, sum_pieces(dkvs[1])], axis=1))
    pieces.append(dkvs[2])
    got += [exchange(d, z, groups) for d in pieces[1:]]
    grad_w = [mm("tf,tm->fm", d, normed1) for d in pieces]
    grad_u = jnp.concatenate([mm("tf,tm->fm", d, unit_low) for d in pieces])
    grad_s = jnp.concatenate([jnp.sum(d.astype(F32), axis=0) for d in pieces])
    grad_gain1 = jnp.sum(w_own.astype(F32) * grad_u, axis=0)
    grad_bias1 = jnp.sum(w_own.astype(F32) * grad_s[:, None], axis=0)

    def of_kind(values, kind):
        starts = ((0, 64, 256), (128, 320, 448), (192, 384, 512))[kind]
        return jnp.concatenate([values[at : at + HEAD_DIM] for at in starts])

    grad_q_b = of_kind(grad_s, 0)
    grad_v_b = of_kind(grad_s, 2)
    (w_a, w_b, w_c) = grad_w
    kinds = [
        jnp.concatenate([w_a[:128], w_b[:64]]),
        jnp.concatenate([w_a[128:192], w_b[64:128], w_c[:64]]),
        jnp.concatenate([w_a[192:256], w_b[128:192], w_c[64:]]),
    ]
    if special:
        early = send_rows(jnp.concatenate([k[:128] for k in kinds]), None, at)
        grad_w = jnp.concatenate([k[128:] for k in kinds])
    else:
        grad_w = jnp.concatenate(kinds)
    grad_normed1 = 0.0
    at_row = 0
    for blocks_got in got:
        size = blocks_got[0].shape[1]
        for k, block in enumerate(blocks_got):
            w = lax.dynamic_index_in_dim(w_all, (z - k) % depth, 0, keepdims=False)
            grad_normed1 = grad_normed1 + mm("tf,fm->tm", block, w[at_row : at_row + size])
        at_row += size
    unit_in, root_in = normalise(wide)
    grad_in = (grad_middle + normalise_back(grad_normed1, unit_in, root_in, gain1)).astype(BF)

    placed_q = lax.dynamic_update_slice(jnp.zeros((model,), F32), grad_q_b, (z * width,))
    placed_v = lax.dynamic_update_slice(jnp.zeros((model,), F32), grad_v_b, (z * width,))
    small_grads = jnp.concatenate(
        [
            v.reshape(shards, -1)
            for v in (
                grad_gain1,
                grad_bias1,
                placed_q,
                placed_v,
                grad_out_b,
                grad_gain2,
                grad_bias2,
                grad_reduce_b,
                grad_expand_b,
            )
        ],
        axis=1,
    )
    if special:
        grad_triple_w, flat = send_triple(grad_w, small_grads, at, early)
    else:
        grad_triple_w, flat = send_triple_whole(grad_w, small_grads, at)
    vecs = [flat[i * here : (i + 1) * here] for i in range(8)]
    grad_e_b = flat[8 * here : 8 * here + hidden_here]
    return (
        result,
        grad_in,
        vecs[0],
        vecs[1],
        grad_triple_w,
        vecs[2],
        vecs[3],
        grad_out_w,
        vecs[4],
        vecs[5],
        vecs[6],
        grad_expand_w,
        grad_e_b,
        grad_reduce_w,
        vecs[7],
    )


def reduce_half(weight, c, half):
    pieces = weight.reshape(-1, 2, half, weight.shape[1])
    return part(pieces, c, 1, 1).reshape(-1, weight.shape[1]).T


def solution(mesh):
    fsdp, seq = mesh.shape["fsdp"], mesh.shape["seq"]
    wide = Mesh(
        mesh.devices.reshape(fsdp // GROUP, GROUP // 2, 2, seq // 2, 2), ("g", "z", "x", "y", "c")
    )
    rows = P(ALL, None)
    vector = P(WEIGHT_AXES)
    matrix = P(None, WEIGHT_AXES)
    return jax.shard_map(
        on_device,
        mesh=wide,
        in_specs=(
            rows,
            rows,
            vector,
            vector,
            matrix,
            vector,
            vector,
            matrix,
            vector,
            vector,
            vector,
            matrix,
            vector,
            matrix,
            vector,
        ),
        out_specs=(
            rows,
            rows,
            vector,
            vector,
            matrix,
            vector,
            vector,
            matrix,
            vector,
            vector,
            vector,
            matrix,
            vector,
            matrix,
            vector,
        ),
        check_vma=False,
    )
```
